128 devices in a mesh: dp: 4 (over z), verts: 32 (over y, x, core).
Axes of the slice: x: 4, y: 4, z: 4, core: 2. Of those that a mesh axis runs over, the one named last changes fastest.
Arguments:
- feats: bfloat16 [4, 32768, 512], P('dp', 'verts'), may hold values from -64 to 64
- weights: bfloat16 [4, 512, 512], replicated, may hold values from -0.25 to 0.25
- grad_out: bfloat16 [4, 32768, 512], P('dp', 'verts'), may hold values from -6 to 6
- neighbours: int32 [512, 8], replicated, may hold values from 0 to 511, as said below
- valid: int32 [512, 64], replicated, may hold values from 0 to 1, as said below
Outputs:
- attn_out: bfloat16 [4, 32768, 512], P('dp', 'verts')
- grad_feats: bfloat16 [4, 32768, 512], P('dp', 'verts')
- grad_weights: float32 [4, 512, 512], P(None, 'dp')
The draws below stay inside these ranges and needn't reach their ends.
Inputs may be any that keep to these rules, and one draw needn't show every extreme that they name: `neighbours`: entry 0 of block b is b; entries 1 to 3 are other blocks of the same partition of 16 blocks (partition b // 16); entries 4 to 7 lie on four different other partitions. The blocks of one partition name exactly 2 distinct blocks of each other partition. A row names no block twice. `valid`: in each block the real vertices come first and are 32 or more.
All inputs are finite; a program needn't handle non-finite values.
Results may differ from the reference program's by a relative error of at most 0.0095.
The reference program's roundings to bfloat16 on the way count: a program that leaves them out, or rounds other values in their place, can miss the bound.
Values may be sent and summed in bfloat16 or wider, within the bound.
No kernel may reach another device: no remote copies, remote signals or barrier semaphores. Data moves between devices by JAX's collectives and lax.ppermute only.
A program may use at most 256 MiB of HBM per device.

```python
import math
import jax
import jax.numpy as jnp
from jax import lax

D = 512
H = 8
BS = 64
NNB = 8
CAP = 2
BLK_DEV = 16
NB = 512
NV = 32768
SUBJECTS = 4
N_VERTS = 32


def draw_feats(key, part):
    shape_all = (SUBJECTS, NV, D)
    result = jnp.clip(jax.random.normal(key, shape_all, jnp.float32), -6.0, 6.0)
    return result.astype(jnp.bfloat16)


def draw_neighbours(key, part):
    key_one, key_two, key_three = jax.random.split(jax.random.fold_in(key, 11), 3)
    nparts = N_VERTS
    orders = jax.vmap(lambda each: jax.random.permutation(each, BLK_DEV))(jax.random.split(key_one, nparts)).astype(jnp.int32)
    places = jnp.argsort(orders, axis=1, stable=True).astype(jnp.int32)
    shifts = jax.random.randint(key_two, (nparts,), 0, nparts - 1).astype(jnp.int32)
    candidates = jax.vmap(lambda each: jax.random.permutation(each, BLK_DEV))(jax.random.split(key_three, nparts * nparts))
    candidates = candidates[:, :CAP].reshape(nparts, nparts, CAP).astype(jnp.int32)
    global_ids = jnp.arange(NB, dtype=jnp.int32)
    part_of = global_ids // BLK_DEV
    local_ids = global_ids % BLK_DEV
    position = places[part_of, local_ids]
    columns = [global_ids]
    for offset in range(1, 4):
        columns.append(orders[part_of, (position + offset) % BLK_DEV] + part_of * BLK_DEV)
    for offset in range(4):
        counter = position * 4 + offset + shifts[part_of]
        hop_size = 1 + counter % (nparts - 1)
        cand_idx = counter // (nparts - 1) % CAP
        peer_part = (part_of + hop_size) % nparts
        columns.append(peer_part * BLK_DEV + candidates[part_of, peer_part, cand_idx])
    return jnp.stack(columns, axis=1).astype(jnp.int32)


def draw_valid(key, part):
    counts = jax.random.randint(jax.random.fold_in(key, 23), (NB, 1), BS // 2, BS + 1).astype(jnp.int32)
    counts = counts.at[0, 0].set(BS // 2)
    return (jnp.arange(BS, dtype=jnp.int32)[None, :] < counts).astype(jnp.int32)


def level_of(stream_key, dims, pieces, low, top_value):
    def one(dim, shards_of):
        heights = jax.random.uniform(jax.random.fold_in(jax.random.fold_in(stream_key, 6), dim), (shards_of,), jnp.float32, low / len(pieces), top_value / len(pieces))
        return jnp.repeat(jnp.exp(heights), dims[dim] // shards_of).reshape((-1,) + (1,) * (len(dims) - dim - 1))

    level = one(*pieces[0])
    for cut in pieces[1:]:
        level = level * one(*cut)
    return level


def noise(own_key, shape, deviation, reach, cuts=(), held_as=jnp.bfloat16):
    values = jax.random.normal(own_key, shape, jnp.float32) * deviation
    if len(cuts) > 0:
        values = level_of(own_key, shape, cuts, -0.22, 0.18) * values
    return jnp.clip(values, min=-reach, max=reach).astype(held_as)


def setup_inputs(seed: int = 0) -> dict:
    key_list = jax.random.split(jax.random.key(seed), 6)
    feats = draw_feats(jax.random.fold_in(key_list[5], 71), 0)
    weights = noise(key_list[1], (4, D, D), D ** -0.5, 0.25)
    grad_out = noise(key_list[2], (SUBJECTS, NV, D), 1.0, 6.0, ((0, 4), (1, 32)))
    neighbours = draw_neighbours(jax.random.fold_in(key_list[5], 71), 0)
    valid = draw_valid(jax.random.fold_in(key_list[5], 71), 0)
    return dict(feats=feats, weights=weights, grad_out=grad_out, neighbours=neighbours, valid=valid)


def block_pass(query_blk, grad_blk, key_blk, value_blk, key_ok, scaling):
    query_f = query_blk.astype(jnp.float32)
    key_f = key_blk.astype(jnp.float32)
    value_f = value_blk.astype(jnp.float32)
    grad_f = grad_blk.astype(jnp.float32)
    scores = jnp.einsum('gqhd,gkhd->ghqk', query_f, key_f) * scaling
    scores = jnp.where(key_ok[:, None, None, :], scores, -jnp.inf)
    row_top = lax.optimization_barrier(jnp.max(scores, axis=-1, keepdims=True))
    raised = jnp.exp(scores - row_top)
    probs_f = raised / lax.optimization_barrier(jnp.sum(raised, axis=-1, keepdims=True))
    probs_r = lax.optimization_barrier(probs_f.astype(jnp.bfloat16)).astype(jnp.float32)
    attended = jnp.einsum('ghqk,gkhd->gqhd', probs_r, value_f).astype(jnp.bfloat16)
    dprob = jnp.einsum('gqhd,gkhd->ghqk', grad_f, value_f)
    inner_sum = lax.optimization_barrier(jnp.sum(probs_f * dprob, axis=-1, keepdims=True))
    dscore = probs_f * (dprob - inner_sum) * scaling
    dscore_r = lax.optimization_barrier(dscore.astype(jnp.bfloat16)).astype(jnp.float32)
    grad_q = jnp.einsum('ghqk,gkhd->gqhd', dscore_r, key_f).astype(jnp.bfloat16)
    grad_keys = jnp.einsum('ghqk,gqhd->gkhd', dscore_r, query_f)
    grad_values = jnp.einsum('ghqk,gqhd->gkhd', probs_r, grad_f)
    return (attended, grad_q, grad_keys, grad_values)

def reference(feats, weights, grad_out, neighbours, valid):
    head_dim = D // H
    scaling = 1.0 / math.sqrt(head_dim)
    all_blocks = neighbours.shape[0]
    groups = all_blocks // 8
    w_kv = jnp.concatenate([weights[1], weights[2]], axis=1)
    usable = valid > 0
    outputs = []
    grads_in = []
    totals_w = jnp.zeros((4, D, D), jnp.float32)
    for subject in range(feats.shape[0]):
        inputs_now = feats[subject]
        cotangent = grad_out[subject]
        queries = jnp.dot(inputs_now, weights[0], preferred_element_type=jnp.float32).astype(jnp.bfloat16)
        key_vals = jnp.dot(inputs_now, w_kv, preferred_element_type=jnp.float32).astype(jnp.bfloat16)
        key_vals = key_vals.reshape(all_blocks, BS, 2 * D)
        upstream = jnp.dot(cotangent, weights[3].T, preferred_element_type=jnp.float32).astype(jnp.bfloat16)
        query_groups = queries.reshape(groups, 8, BS, H, head_dim)
        grad_groups = upstream.reshape(groups, 8, BS, H, head_dim)
        entry_groups = neighbours.reshape(groups, 8, NNB)

        def group_step(totals, inputs):
            query_blk, grad_blk, entries = inputs
            flat_ids = entries.reshape(-1)
            fetched = key_vals[flat_ids].reshape(8, NNB * BS, 2, H, head_dim)
            key_ok = usable[flat_ids].reshape(8, NNB * BS)
            attended, grad_q, grad_keys, grad_values = block_pass(query_blk, grad_blk, fetched[:, :, 0], fetched[:, :, 1], key_ok, scaling)
            both_grads = jnp.stack([grad_keys, grad_values], axis=2).reshape(8 * NNB, BS, 2 * D)
            return (totals.at[flat_ids].add(both_grads), (attended, grad_q))
        start_tot = jnp.zeros((all_blocks, BS, 2 * D), jnp.float32)
        totals, (attended, grad_q) = lax.scan(group_step, start_tot, (query_groups, grad_groups, entry_groups))
        attended = attended.reshape(all_blocks * BS, D)
        grad_q = grad_q.reshape(all_blocks * BS, D)
        grad_kv = totals.reshape(all_blocks * BS, 2 * D).astype(jnp.bfloat16)
        outputs.append(jnp.dot(attended, weights[3], preferred_element_type=jnp.float32).astype(jnp.bfloat16))
        grad_sum = jnp.dot(grad_q, weights[0].T, preferred_element_type=jnp.float32) + jnp.dot(grad_kv, w_kv.T, preferred_element_type=jnp.float32)
        grads_in.append(grad_sum.astype(jnp.bfloat16))
        grad_wkv = jnp.dot(inputs_now.T, grad_kv, preferred_element_type=jnp.float32)
        terms = jnp.stack([jnp.dot(inputs_now.T, grad_q, preferred_element_type=jnp.float32), grad_wkv[:, :D], grad_wkv[:, D:], jnp.dot(attended.T, cotangent, preferred_element_type=jnp.float32)])
        totals_w = totals_w + terms
    return (jnp.stack(outputs), jnp.stack(grads_in), totals_w)
```

```python
import functools
import math

import jax
import jax.numpy as jnp
from jax import lax
from jax.experimental import pallas as pl
from jax.experimental.pallas import tpu as pltpu
from jax.sharding import PartitionSpec as P

H = 8
BS = 64
NNB = 8
CAP = 2

ROWS = 512
HALF = 256

NT = (((1,), (1,)), ((), ()))
TN = (((0,), (0,)), ((), ()))


def dot(a, b):
    return jnp.dot(a, b, preferred_element_type=jnp.float32)


def dot_nt(a, b):
    return lax.dot_general(a, b, NT, preferred_element_type=jnp.float32)


def dot_tn(a, b):
    return lax.dot_general(a, b, TN, preferred_element_type=jnp.float32)


def layer_kernel(
    steps_a,
    steps_b,
    remote,
    scaling,
    entries,
    counts,
    far_ref,
    own_kv_ref,
    wkv_ref,
    q_ref,
    u_ref,
    diag_ref,
    att_ref,
    gq_ref,
    gkv_ref,
    back_ref,
    keys,
    values,
    gkeys,
    gvalues,
):
    step = pl.program_id(0)
    per = ROWS // BS
    own = own_kv_ref.shape[0] // BS
    dim = q_ref.shape[1]

    @pl.when(step == 0)
    def _():
        for b in range(own):
            rows = slice(b * BS, (b + 1) * BS)
            keys[remote + b] = own_kv_ref[rows, :dim]
            values[remote + b] = own_kv_ref[rows, dim:]
            gkeys[remote + b] = jnp.zeros((BS, dim), jnp.float32)
            gvalues[remote + b] = jnp.zeros((BS, dim), jnp.float32)

    @pl.when(step < steps_a)
    def _():
        first = pl.ds(step * per, per)
        both = dot(far_ref[...], wkv_ref[...]).astype(jnp.bfloat16)
        keys[first] = both[:, :dim].reshape(per, BS, dim)
        values[first] = both[:, dim:].reshape(per, BS, dim)
        gkeys[first] = jnp.zeros((per, BS, dim), jnp.float32)
        gvalues[first] = jnp.zeros((per, BS, dim), jnp.float32)

    @pl.when((step >= steps_a) & (step < steps_a + steps_b))
    def _():
        base = (step - steps_a) * NNB
        ids = [entries[base + n] for n in range(NNB)]
        ends = [counts[base + n] for n in range(NNB)]
        place = lax.broadcasted_iota(jnp.int32, (BS, HALF), 0)
        lane_head = lax.broadcasted_iota(jnp.int32, (BS, HALF), 1) // BS
        queries = q_ref[...] * jnp.bfloat16(scaling)
        ups = u_ref[...]
        for half in range(dim // HALF):
            cols = slice(half * HALF, (half + 1) * HALF)
            diag = diag_ref[...]
            qbd = jnp.concatenate([queries[:, cols]] * (HALF // BS), axis=0) * diag
            ubd = jnp.concatenate([ups[:, cols]] * (HALF // BS), axis=0) * diag
            k_all = jnp.concatenate([keys[i, :, cols] for i in ids], axis=0)
            v_all = jnp.concatenate([values[i, :, cols] for i in ids], axis=0)
            scores = dot_nt(k_all, qbd)
            scores = jnp.concatenate(
                [
                    jnp.where(place < ends[n], scores[n * BS : (n + 1) * BS], -1e30)
                    for n in range(NNB)
                ],
                axis=0,
            )
            top = jnp.max(scores, axis=0, keepdims=True)
            raised = jnp.exp(scores - top)
            probs = raised * (1.0 / jnp.sum(raised, axis=0, keepdims=True))
            probs_b = probs.astype(jnp.bfloat16)
            dprob = dot_nt(v_all, ubd)
            inner = jnp.sum(probs * dprob, axis=0, keepdims=True)
            dscore = (probs * (dprob - inner)).astype(jnp.bfloat16)
            att_all = dot_tn(probs_b, v_all)
            gq_all = dot_tn(dscore, k_all)
            att = att_all[:BS]
            gq = gq_all[:BS]
            for h in range(1, HALF // BS):
                rows = slice(h * BS, (h + 1) * BS)
                att = jnp.where(lane_head == h, att_all[rows], att)
                gq = jnp.where(lane_head == h, gq_all[rows], gq)
            att_ref[:, cols] = att.astype(jnp.bfloat16)
            gq_ref[:, cols] = (gq * scaling).astype(jnp.bfloat16)
            grad_v = dot(probs_b, ubd)
            grad_k = dot(dscore, qbd)
            for n in range(NNB):
                rows = slice(n * BS, (n + 1) * BS)
                gkeys[ids[n], :, cols] += grad_k[rows]
                gvalues[ids[n], :, cols] += grad_v[rows]

    @pl.when(step >= steps_a + steps_b)
    def _():
        chunk = step - steps_a - steps_b
        first = pl.ds(chunk * per, per)
        gkv_ref[:, :dim] = gkeys[first].reshape(ROWS, dim).astype(jnp.bfloat16)
        gkv_ref[:, dim:] = gvalues[first].reshape(ROWS, dim).astype(jnp.bfloat16)

        @pl.when(chunk < steps_a)
        def _():
            back_ref[...] = dot_nt(gkv_ref[...], wkv_ref[...]).astype(jnp.bfloat16)


def layer_call(entries, counts, far, own_kv, wkv, queries, ups, scaling):
    far_rows, dim = far.shape
    rows = queries.shape[0]
    blocks = rows // BS
    steps_a = far_rows // ROWS
    steps_c = (far_rows + rows) // ROWS
    steps_b = blocks
    table = (far_rows + rows) // BS
    head = jnp.arange(HALF, dtype=jnp.int32) // BS
    diag = (head[:, None] == head[None, :]).astype(jnp.bfloat16)

    def at_b(i, *_):
        return (jnp.clip(i - steps_a, 0, steps_b - 1), 0)

    def at_c(i, *_):
        return (jnp.maximum(i - steps_a - steps_b, 0), 0)

    def at_back(i, *_):
        return (jnp.clip(i - steps_a - steps_b, 0, steps_a - 1), 0)

    def whole(shape):
        return pl.BlockSpec(shape, lambda i, *_: (0, 0))

    return pl.pallas_call(
        functools.partial(layer_kernel, steps_a, steps_b, far_rows // BS, scaling),
        grid_spec=pltpu.PrefetchScalarGridSpec(
            num_scalar_prefetch=2,
            grid=(steps_a + steps_b + steps_c,),
            in_specs=[
                pl.BlockSpec((ROWS, dim), lambda i, *_: (jnp.minimum(i, steps_a - 1), 0)),
                whole((rows, 2 * dim)),
                whole((dim, 2 * dim)),
                pl.BlockSpec((BS, dim), at_b),
                pl.BlockSpec((BS, dim), at_b),
                whole((HALF, HALF)),
            ],
            out_specs=[
                pl.BlockSpec((BS, dim), at_b),
                pl.BlockSpec((BS, dim), at_b),
                pl.BlockSpec((ROWS, 2 * dim), at_c),
                pl.BlockSpec((ROWS, dim), at_back),
            ],
            scratch_shapes=[
                pltpu.VMEM((table, BS, dim), jnp.bfloat16),
                pltpu.VMEM((table, BS, dim), jnp.bfloat16),
                pltpu.VMEM((table, BS, dim), jnp.float32),
                pltpu.VMEM((table, BS, dim), jnp.float32),
            ],
        ),
        out_shape=[
            jax.ShapeDtypeStruct((rows, dim), jnp.bfloat16),
            jax.ShapeDtypeStruct((rows, dim), jnp.bfloat16),
            jax.ShapeDtypeStruct((far_rows + rows, 2 * dim), jnp.bfloat16),
            jax.ShapeDtypeStruct((far_rows, dim), jnp.bfloat16),
        ],
        compiler_params=pltpu.CompilerParams(vmem_limit_bytes=56 * 2**20),
    )(entries, counts, far, own_kv, wkv, queries, ups, diag)


def combine_kernel(per, send_ref, base_ref, ret_ref, out_ref, acc):
    step = pl.program_id(0)

    @pl.when(step == 0)
    def _():
        acc[...] = base_ref[...]

    for i in range(per):
        acc[send_ref[step * per + i]] += ret_ref[i].astype(jnp.float32)

    @pl.when(step == pl.num_programs(0) - 1)
    def _():
        out_ref[...] = acc[...].astype(jnp.bfloat16)


def combine_call(send, base, returned):
    blocks, _, dim = base.shape
    total = returned.shape[0]
    per = 8
    return pl.pallas_call(
        functools.partial(combine_kernel, per),
        grid_spec=pltpu.PrefetchScalarGridSpec(
            num_scalar_prefetch=1,
            grid=(total // per,),
            in_specs=[
                pl.BlockSpec((blocks, BS, dim), lambda i, *_: (0, 0, 0)),
                pl.BlockSpec((per, BS, dim), lambda i, *_: (i, 0, 0)),
            ],
            out_specs=pl.BlockSpec((blocks, BS, dim), lambda i, *_: (0, 0, 0)),
            scratch_shapes=[pltpu.VMEM((blocks, BS, dim), jnp.float32)],
        ),
        out_shape=jax.ShapeDtypeStruct((blocks, BS, dim), jnp.bfloat16),
        compiler_params=pltpu.CompilerParams(vmem_limit_bytes=32 * 2**20),
    )(send, base, returned)


def local(feats, weights, grad_out, neighbours, valid):
    nparts = lax.axis_size("verts")
    me = lax.axis_index("verts")
    _, rows, dim = feats.shape
    blocks = rows // BS
    scaling = 1.0 / math.sqrt(dim // H)
    part_ids = jnp.arange(nparts, dtype=jnp.int32)
    inputs_now = feats[0]
    cotangent = grad_out[0]
    w_kv = jnp.concatenate([weights[1], weights[2]], axis=1)

    theirs = neighbours.reshape(nparts, blocks * NNB)
    mine = (theirs // blocks == me) & (part_ids[:, None] != me)
    place = theirs % blocks
    low = jnp.min(jnp.where(mine, place, blocks), axis=1)
    high = jnp.max(jnp.where(mine, place, -1), axis=1)
    send = jnp.stack([low % blocks, jnp.maximum(high, 0)], axis=1).reshape(-1)

    lists = lax.dynamic_slice_in_dim(neighbours, me * blocks, blocks, 0).reshape(-1)
    owner = lists // blocks
    named = owner[:, None] == part_ids[None, :]
    lower = jnp.min(jnp.where(named, (lists % blocks)[:, None], blocks), axis=0)
    slot = (jnp.sum(jnp.where(named, lower[None, :], 0), axis=1) != lists % blocks).astype(jnp.int32)
    entries = jnp.where(owner == me, nparts * CAP + lists % blocks, owner * CAP + slot)
    counts = jnp.sum(valid, axis=1)[lists]

    far = lax.all_to_all(
        inputs_now.reshape(blocks, BS, dim)[send].reshape(nparts, CAP, BS, dim),
        "verts",
        split_axis=0,
        concat_axis=0,
        tiled=True,
    ).reshape(nparts * CAP * BS, dim)

    queries = dot(inputs_now, weights[0]).astype(jnp.bfloat16)
    ups = dot_nt(cotangent, weights[3]).astype(jnp.bfloat16)
    own_kv = dot(inputs_now, w_kv).astype(jnp.bfloat16)

    attended, grad_q, grad_kv, back = layer_call(
        entries, counts, far, own_kv, w_kv, queries, ups, scaling
    )
    returned = lax.all_to_all(
        back.reshape(nparts, CAP, BS, dim), "verts", split_axis=0, concat_axis=0, tiled=True
    ).reshape(nparts * CAP, BS, dim)

    attn_out = dot(attended, weights[3]).astype(jnp.bfloat16)
    own_grad = grad_kv[nparts * CAP * BS :]
    base = dot_nt(grad_q, weights[0]) + dot_nt(own_grad, w_kv)
    grad_wkv = dot_tn(inputs_now, own_grad) + dot_tn(far, grad_kv[: nparts * CAP * BS])
    terms = jnp.stack(
        [
            dot_tn(inputs_now, grad_q),
            grad_wkv[:, :dim],
            grad_wkv[:, dim:],
            dot_tn(attended, cotangent),
        ]
    )
    shared = lax.psum_scatter(terms, "dp", scatter_dimension=1, tiled=True)
    flat = shared.reshape(-1, dim)
    pieces = lax.psum_scatter(flat, "verts", scatter_dimension=0, tiled=True)
    grad_weights = lax.all_gather(pieces, "verts", axis=0, tiled=True).reshape(shared.shape)

    grad_feats = combine_call(send, base.reshape(blocks, BS, dim), returned)
    return (attn_out[None], grad_feats.reshape(1, rows, dim), grad_weights)


def solution(mesh):
    in_specs = (P("dp", "verts", None), P(), P("dp", "verts", None), P(), P())
    out_specs = (P("dp", "verts", None), P("dp", "verts", None), P(None, "dp", None))
    return jax.shard_map(local, mesh=mesh, in_specs=in_specs, out_specs=out_specs, check_vma=False)
```

```python
import functools
import math

import jax
import jax.numpy as jnp
from jax import lax
from jax.experimental import pallas as pl
from jax.experimental.pallas import tpu as pltpu
from jax.sharding import PartitionSpec as P

H = 8
BS = 64
NNB = 8
CAP = 2

ROWS = 512
HALF = 256

NT = (((1,), (1,)), ((), ()))
TN = (((0,), (0,)), ((), ()))


def dot(a, b):
    return jnp.dot(a, b, preferred_element_type=jnp.float32)


def dot_nt(a, b):
    return lax.dot_general(a, b, NT, preferred_element_type=jnp.float32)


def dot_tn(a, b):
    return lax.dot_general(a, b, TN, preferred_element_type=jnp.float32)


def layer_kernel(
    steps_a,
    steps_b,
    remote,
    scaling,
    entries,
    counts,
    far_ref,
    own_ref,
    cot_ref,
    own_kv_ref,
    wkv_ref,
    q_ref,
    u_ref,
    diag_ref,
    att_ref,
    gq_ref,
    own_grad_ref,
    back_ref,
    qo_ref,
    kv_ref,
    keys,
    values,
    gkeys,
    gvalues,
    att_all,
    gq_all,
):
    step = pl.program_id(0)
    per = ROWS // BS
    own = own_kv_ref.shape[0] // BS
    dim = q_ref.shape[1]

    @pl.when(step == 0)
    def _():
        for b in range(own):
            rows = slice(b * BS, (b + 1) * BS)
            keys[remote + b] = own_kv_ref[rows, :dim]
            values[remote + b] = own_kv_ref[rows, dim:]
            gkeys[remote + b] = jnp.zeros((BS, dim), jnp.float32)
            gvalues[remote + b] = jnp.zeros((BS, dim), jnp.float32)

    @pl.when(step < steps_a)
    def _():
        first = pl.ds(step * per, per)
        both = dot(far_ref[...], wkv_ref[...]).astype(jnp.bfloat16)
        keys[first] = both[:, :dim].reshape(per, BS, dim)
        values[first] = both[:, dim:].reshape(per, BS, dim)
        gkeys[first] = jnp.zeros((per, BS, dim), jnp.float32)
        gvalues[first] = jnp.zeros((per, BS, dim), jnp.float32)

    @pl.when((step >= steps_a) & (step < steps_a + steps_b))
    def _():
        block = step - steps_a
        base = block * NNB
        ids = [entries[base + n] for n in range(NNB)]
        ends = [counts[base + n] for n in range(NNB)]
        place = lax.broadcasted_iota(jnp.int32, (BS, HALF), 0)
        lane_head = lax.broadcasted_iota(jnp.int32, (BS, HALF), 1) // BS
        queries = q_ref[...] * jnp.bfloat16(scaling)
        ups = u_ref[...]
        for half in range(dim // HALF):
            cols = slice(half * HALF, (half + 1) * HALF)
            diag = diag_ref[...]
            qbd = jnp.concatenate([queries[:, cols]] * (HALF // BS), axis=0) * diag
            ubd = jnp.concatenate([ups[:, cols]] * (HALF // BS), axis=0) * diag
            k_all = jnp.concatenate([keys[i, :, cols] for i in ids], axis=0)
            v_all = jnp.concatenate([values[i, :, cols] for i in ids], axis=0)
            scores = dot_nt(k_all, qbd)
            scores = jnp.concatenate(
                [
                    jnp.where(place < ends[n], scores[n * BS : (n + 1) * BS], -1e30)
                    for n in range(NNB)
                ],
                axis=0,
            )
            top = jnp.max(scores, axis=0, keepdims=True)
            raised = jnp.exp(scores - top)
            probs = raised * (1.0 / jnp.sum(raised, axis=0, keepdims=True))
            probs_b = probs.astype(jnp.bfloat16)
            dprob = dot_nt(v_all, ubd)
            inner = jnp.sum(probs * dprob, axis=0, keepdims=True)
            dscore = (probs * (dprob - inner)).astype(jnp.bfloat16)
            att_wide = dot_tn(probs_b, v_all)
            gq_wide = dot_tn(dscore, k_all)
            att = att_wide[:BS]
            gq = gq_wide[:BS]
            for h in range(1, HALF // BS):
                rows = slice(h * BS, (h + 1) * BS)
                att = jnp.where(lane_head == h, att_wide[rows], att)
                gq = jnp.where(lane_head == h, gq_wide[rows], gq)
            att = att.astype(jnp.bfloat16)
            gq = (gq * scaling).astype(jnp.bfloat16)
            att_ref[:, cols] = att
            gq_ref[:, cols] = gq
            att_all[block, :, cols] = att
            gq_all[block, :, cols] = gq
            grad_v = dot(probs_b, ubd)
            grad_k = dot(dscore, qbd)
            for n in range(NNB):
                rows = slice(n * BS, (n + 1) * BS)
                gkeys[ids[n], :, cols] += grad_k[rows]
                gvalues[ids[n], :, cols] += grad_v[rows]

    @pl.when(step >= steps_a + steps_b)
    def _():
        chunk = step - steps_a - steps_b
        first = pl.ds(chunk * per, per)
        grad_k = gkeys[first].reshape(ROWS, dim).astype(jnp.bfloat16)
        grad_v = gvalues[first].reshape(ROWS, dim).astype(jnp.bfloat16)

        @pl.when(chunk == 0)
        def _():
            kv_ref[...] = jnp.zeros_like(kv_ref)
            qo_ref[...] = jnp.zeros_like(qo_ref)

        @pl.when(chunk < steps_a)
        def _():
            back_ref[...] = (
                dot_nt(grad_k, wkv_ref[:, :dim]) + dot_nt(grad_v, wkv_ref[:, dim:])
            ).astype(jnp.bfloat16)
            kv_ref[0] += dot_tn(far_ref[...], grad_k)
            kv_ref[1] += dot_tn(far_ref[...], grad_v)

        @pl.when(chunk >= steps_a)
        def _():
            own_grad_ref[:, :dim] = grad_k
            own_grad_ref[:, dim:] = grad_v
            here = pl.ds((chunk - steps_a) * per, per)
            kv_ref[0] += dot_tn(own_ref[...], grad_k)
            kv_ref[1] += dot_tn(own_ref[...], grad_v)
            qo_ref[0] += dot_tn(own_ref[...], gq_all[here].reshape(ROWS, dim))
            qo_ref[1] += dot_tn(att_all[here].reshape(ROWS, dim), cot_ref[...])


def layer_call(entries, counts, far, own, cot, own_kv, wkv, queries, ups, scaling):
    far_rows, dim = far.shape
    rows = queries.shape[0]
    blocks = rows // BS
    steps_a = far_rows // ROWS
    steps_c = (far_rows + rows) // ROWS
    steps_b = blocks
    table = (far_rows + rows) // BS
    head = jnp.arange(HALF, dtype=jnp.int32) // BS
    diag = (head[:, None] == head[None, :]).astype(jnp.bfloat16)

    def at_far(i, *_):
        return (jnp.where(i < steps_a + steps_b, jnp.minimum(i, steps_a - 1), jnp.minimum(i - steps_a - steps_b, steps_a - 1)), 0)

    def at_b(i, *_):
        return (jnp.clip(i - steps_a, 0, steps_b - 1), 0)

    def at_own(i, *_):
        return (jnp.maximum(i - 2 * steps_a - steps_b, 0), 0)

    def at_back(i, *_):
        return (jnp.clip(i - steps_a - steps_b, 0, steps_a - 1), 0)

    def whole(shape):
        return pl.BlockSpec(shape, lambda i, *_: (0,) * len(shape), pipeline_mode=pl.Buffered(1))

    return pl.pallas_call(
        functools.partial(layer_kernel, steps_a, steps_b, far_rows // BS, scaling),
        grid_spec=pltpu.PrefetchScalarGridSpec(
            num_scalar_prefetch=2,
            grid=(steps_a + steps_b + steps_c,),
            in_specs=[
                pl.BlockSpec((ROWS, dim), at_far),
                pl.BlockSpec((ROWS, dim), at_own),
                pl.BlockSpec((ROWS, dim), at_own),
                whole((rows, 2 * dim)),
                whole((dim, 2 * dim)),
                pl.BlockSpec((BS, dim), at_b),
                pl.BlockSpec((BS, dim), at_b),
                whole((HALF, HALF)),
            ],
            out_specs=[
                pl.BlockSpec((BS, dim), at_b),
                pl.BlockSpec((BS, dim), at_b),
                pl.BlockSpec((ROWS, 2 * dim), at_own),
                pl.BlockSpec((ROWS, dim), at_back),
                pl.BlockSpec((2, dim, dim), lambda i, *_: (0, 0, 0)),
                pl.BlockSpec((2, dim, dim), lambda i, *_: (0, 0, 0)),
            ],
            scratch_shapes=[
                pltpu.VMEM((table, BS, dim), jnp.bfloat16),
                pltpu.VMEM((table, BS, dim), jnp.bfloat16),
                pltpu.VMEM((table, BS, dim), jnp.float32),
                pltpu.VMEM((table, BS, dim), jnp.float32),
                pltpu.VMEM((blocks, BS, dim), jnp.bfloat16),
                pltpu.VMEM((blocks, BS, dim), jnp.bfloat16),
            ],
        ),
        out_shape=[
            jax.ShapeDtypeStruct((rows, dim), jnp.bfloat16),
            jax.ShapeDtypeStruct((rows, dim), jnp.bfloat16),
            jax.ShapeDtypeStruct((rows, 2 * dim), jnp.bfloat16),
            jax.ShapeDtypeStruct((far_rows, dim), jnp.bfloat16),
            jax.ShapeDtypeStruct((2, dim, dim), jnp.float32),
            jax.ShapeDtypeStruct((2, dim, dim), jnp.float32),
        ],
        compiler_params=pltpu.CompilerParams(vmem_limit_bytes=58 * 2**20),
    )(entries, counts, far, own, cot, own_kv, wkv, queries, ups, diag)


def combine_kernel(per, send_ref, base_ref, ret_ref, out_ref, acc):
    step = pl.program_id(0)

    @pl.when(step == 0)
    def _():
        acc[...] = base_ref[...]

    for i in range(per):
        acc[send_ref[step * per + i]] += ret_ref[i].astype(jnp.float32)

    @pl.when(step == pl.num_programs(0) - 1)
    def _():
        out_ref[...] = acc[...].astype(jnp.bfloat16)


def combine_call(send, base, returned):
    blocks, _, dim = base.shape
    total = returned.shape[0]
    per = 8
    return pl.pallas_call(
        functools.partial(combine_kernel, per),
        grid_spec=pltpu.PrefetchScalarGridSpec(
            num_scalar_prefetch=1,
            grid=(total // per,),
            in_specs=[
                pl.BlockSpec((blocks, BS, dim), lambda i, *_: (0, 0, 0)),
                pl.BlockSpec((per, BS, dim), lambda i, *_: (i, 0, 0)),
            ],
            out_specs=pl.BlockSpec((blocks, BS, dim), lambda i, *_: (0, 0, 0)),
            scratch_shapes=[pltpu.VMEM((blocks, BS, dim), jnp.float32)],
        ),
        out_shape=jax.ShapeDtypeStruct((blocks, BS, dim), jnp.bfloat16),
        compiler_params=pltpu.CompilerParams(vmem_limit_bytes=32 * 2**20),
    )(send, base, returned)


def sum_weights(qo_terms, kv_terms, nparts, me, returned):
    first = me % 2 == 0
    up = [(v, v + 1) for v in range(0, nparts, 2)]
    down = [(v + 1, v) for v in range(0, nparts, 2)]
    qo_other = lax.ppermute(qo_terms, "verts", down)
    kv_other = lax.ppermute(kv_terms, "verts", up)
    half = jnp.where(first, qo_terms + qo_other, kv_terms + kv_other)
    half = lax.psum_scatter(half, "dp", scatter_dimension=1, tiled=True)
    half, returned = lax.optimization_barrier((half, returned))
    pair, rows, dim = half.shape
    chips = nparts // 2
    groups = [list(range(c, nparts, 2)) for c in range(2)]
    piece = pair * rows // chips
    parts = lax.all_to_all(
        half.reshape(chips, piece, dim).astype(jnp.bfloat16),
        "verts",
        split_axis=0,
        concat_axis=0,
        axis_index_groups=groups,
        tiled=True,
    )
    total = jnp.sum(parts.astype(jnp.float32), axis=0).astype(jnp.bfloat16)
    whole = lax.all_to_all(
        jnp.broadcast_to(total[None], (chips, piece, dim)),
        "verts",
        split_axis=0,
        concat_axis=0,
        axis_index_groups=groups,
        tiled=True,
    ).reshape(pair, rows, dim)
    other = lax.ppermute(whole, "verts", up + down)
    q_o = jnp.where(first, whole, other).astype(jnp.float32)
    k_v = jnp.where(first, other, whole).astype(jnp.float32)
    return jnp.concatenate([q_o[:1], k_v, q_o[1:]], axis=0), returned


def local(feats, weights, grad_out, neighbours, valid):
    nparts = lax.axis_size("verts")
    me = lax.axis_index("verts")
    _, rows, dim = feats.shape
    blocks = rows // BS
    scaling = 1.0 / math.sqrt(dim // H)
    part_ids = jnp.arange(nparts, dtype=jnp.int32)
    inputs_now = feats[0]
    cotangent = grad_out[0]
    w_kv = jnp.concatenate([weights[1], weights[2]], axis=1)

    theirs = neighbours.reshape(nparts, blocks * NNB)
    mine = (theirs // blocks == me) & (part_ids[:, None] != me)
    place = theirs % blocks
    low = jnp.min(jnp.where(mine, place, blocks), axis=1)
    high = jnp.max(jnp.where(mine, place, -1), axis=1)
    send = jnp.stack([low % blocks, jnp.maximum(high, 0)], axis=1).reshape(-1)

    lists = lax.dynamic_slice_in_dim(neighbours, me * blocks, blocks, 0).reshape(-1)
    owner = lists // blocks
    named = owner[:, None] == part_ids[None, :]
    lower = jnp.min(jnp.where(named, (lists % blocks)[:, None], blocks), axis=0)
    slot = (jnp.sum(jnp.where(named, lower[None, :], 0), axis=1) != lists % blocks).astype(jnp.int32)
    entries = jnp.where(owner == me, nparts * CAP + lists % blocks, owner * CAP + slot)
    counts = jnp.sum(valid, axis=1)[lists]

    far = lax.all_to_all(
        inputs_now.reshape(blocks, BS, dim)[send].reshape(nparts, CAP, BS, dim),
        "verts",
        split_axis=0,
        concat_axis=0,
        tiled=True,
    ).reshape(nparts * CAP * BS, dim)

    queries = dot(inputs_now, weights[0]).astype(jnp.bfloat16)
    ups = dot_nt(cotangent, weights[3]).astype(jnp.bfloat16)
    own_kv = dot(inputs_now, w_kv).astype(jnp.bfloat16)

    attended, grad_q, own_grad, back, qo_terms, kv_terms = layer_call(
        entries, counts, far, inputs_now, cotangent, own_kv, w_kv, queries, ups, scaling
    )
    returned = lax.all_to_all(
        back.reshape(nparts, CAP, BS, dim), "verts", split_axis=0, concat_axis=0, tiled=True
    ).reshape(nparts * CAP, BS, dim)

    attn_out = dot(attended, weights[3]).astype(jnp.bfloat16)
    base = dot_nt(grad_q, weights[0]) + dot_nt(own_grad, w_kv)
    grad_weights, returned = sum_weights(qo_terms, kv_terms, nparts, me, returned)

    grad_feats = combine_call(send, base.reshape(blocks, BS, dim), returned)
    return (attn_out[None], grad_feats.reshape(1, rows, dim), grad_weights)


def solution(mesh):
    in_specs = (P("dp", "verts", None), P(), P("dp", "verts", None), P(), P())
    out_specs = (P("dp", "verts", None), P("dp", "verts", None), P(None, "dp", None))
    return jax.shard_map(local, mesh=mesh, in_specs=in_specs, out_specs=out_specs, check_vma=False)
```

```python
import functools
import math

import jax
import jax.numpy as jnp
from jax import lax
from jax.experimental import pallas as pl
from jax.experimental.pallas import tpu as pltpu
from jax.sharding import PartitionSpec as P

H = 8
BS = 64
NNB = 8
CAP = 2

ROWS = 1024
PAIR = 4
HALF = 256

NT = (((1,), (1,)), ((), ()))
TN = (((0,), (0,)), ((), ()))


def dot(a, b):
    return jnp.dot(a, b, preferred_element_type=jnp.float32)


def dot_nt(a, b):
    return lax.dot_general(a, b, NT, preferred_element_type=jnp.float32)


def dot_tn(a, b):
    return lax.dot_general(a, b, TN, preferred_element_type=jnp.float32)


def layer_kernel(
    steps_a,
    steps_b,
    remote,
    scaling,
    entries,
    counts,
    far_ref,
    own_kv_ref,
    wkv_ref,
    q_ref,
    u_ref,
    diag_ref,
    att_ref,
    gq_ref,
    far_grad_ref,
    own_grad_ref,
    back_ref,
    keys,
    values,
    gkeys,
    gvalues,
):
    step = pl.program_id(0)
    per = ROWS // BS
    own = own_kv_ref.shape[0] // BS
    dim = q_ref.shape[1]

    @pl.when(step == 0)
    def _():
        for b in range(own):
            rows = slice(b * BS, (b + 1) * BS)
            keys[remote + b] = own_kv_ref[rows, :dim]
            values[remote + b] = own_kv_ref[rows, dim:]
            gkeys[remote + b] = jnp.zeros((BS, dim), jnp.float32)
            gvalues[remote + b] = jnp.zeros((BS, dim), jnp.float32)

    @pl.when(step < steps_a)
    def _():
        first = pl.ds(step * per, per)
        both = dot(far_ref[...].reshape(ROWS, dim), wkv_ref[...]).astype(jnp.bfloat16)
        keys[first] = both[:, :dim].reshape(per, BS, dim)
        values[first] = both[:, dim:].reshape(per, BS, dim)
        gkeys[first] = jnp.zeros((per, BS, dim), jnp.float32)
        gvalues[first] = jnp.zeros((per, BS, dim), jnp.float32)

    @pl.when((step >= steps_a) & (step < steps_a + steps_b))
    def _():
        place = lax.broadcasted_iota(jnp.int32, (BS, HALF), 0)
        lane_head = lax.broadcasted_iota(jnp.int32, (BS, HALF), 1) // BS
        diag = diag_ref[...]

        def first_half(sub, half):
            at = slice(sub * BS, (sub + 1) * BS)
            cols = slice(half * HALF, (half + 1) * HALF)
            base = ((step - steps_a) * PAIR + sub) * NNB
            ids = [entries[base + n] for n in range(NNB)]
            ends = [counts[base + n] for n in range(NNB)]
            queries = q_ref[at, cols] * jnp.bfloat16(scaling)
            qbd = jnp.concatenate([queries] * (HALF // BS), axis=0) * diag
            ubd = jnp.concatenate([u_ref[at, cols]] * (HALF // BS), axis=0) * diag
            k_all = jnp.concatenate([keys[i, :, cols] for i in ids], axis=0)
            v_all = jnp.concatenate([values[i, :, cols] for i in ids], axis=0)
            return at, cols, ids, ends, qbd, ubd, k_all, v_all, dot_nt(k_all, qbd), dot_nt(v_all, ubd)

        def second_half(at, cols, ids, ends, qbd, ubd, k_all, v_all, scores, dprob):
            scores = jnp.concatenate(
                [
                    jnp.where(place < ends[n], scores[n * BS : (n + 1) * BS], -1e30)
                    for n in range(NNB)
                ],
                axis=0,
            )
            top = jnp.max(scores, axis=0, keepdims=True)
            raised = jnp.exp(scores - top)
            probs = raised * (1.0 / jnp.sum(raised, axis=0, keepdims=True))
            probs_b = probs.astype(jnp.bfloat16)
            inner = jnp.sum(probs * dprob, axis=0, keepdims=True)
            dscore = (probs * (dprob - inner)).astype(jnp.bfloat16)
            grad_v = dot(probs_b, ubd)
            grad_k = dot(dscore, qbd)
            att_wide = dot_tn(probs_b, v_all)
            gq_wide = dot_tn(dscore, k_all)
            att = att_wide[:BS]
            gq = gq_wide[:BS]
            for h in range(1, HALF // BS):
                rows = slice(h * BS, (h + 1) * BS)
                att = jnp.where(lane_head == h, att_wide[rows], att)
                gq = jnp.where(lane_head == h, gq_wide[rows], gq)
            att_ref[at, cols] = att.astype(jnp.bfloat16)
            gq_ref[at, cols] = (gq * scaling).astype(jnp.bfloat16)
            for n in range(NNB):
                rows = slice(n * BS, (n + 1) * BS)
                gkeys[ids[n], :, cols] += grad_k[rows]
                gvalues[ids[n], :, cols] += grad_v[rows]

        todo = [(sub, half) for sub in range(PAIR) for half in range(dim // HALF)]
        held = first_half(*todo[0])
        for after in todo[1:] + [None]:
            ahead = first_half(*after) if after else None
            second_half(*held)
            held = ahead

    @pl.when(step >= steps_a + steps_b)
    def _():
        chunk = step - steps_a - steps_b
        first = pl.ds(chunk * per, per)
        grad_k = gkeys[first].reshape(ROWS, dim).astype(jnp.bfloat16)
        grad_v = gvalues[first].reshape(ROWS, dim).astype(jnp.bfloat16)

        @pl.when(chunk < steps_a)
        def _():
            far_grad_ref[:, :dim] = grad_k
            far_grad_ref[:, dim:] = grad_v
            back = dot_nt(grad_k, wkv_ref[:, :dim]) + dot_nt(grad_v, wkv_ref[:, dim:])
            back_ref[...] = back.astype(jnp.bfloat16).reshape(per, BS, dim)

        @pl.when(chunk >= steps_a)
        def _():
            own_grad_ref[:, :dim] = grad_k
            own_grad_ref[:, dim:] = grad_v


def layer_call(entries, counts, far, own_kv, wkv, queries, ups, scaling):
    parts, _, _, dim = far.shape
    far_rows = parts * CAP * BS
    rows = queries.shape[0]
    blocks = rows // BS
    steps_a = far_rows // ROWS
    steps_c = (far_rows + rows) // ROWS
    steps_b = blocks // PAIR
    table = (far_rows + rows) // BS
    half = steps_a // CAP
    per = ROWS // BS
    head = jnp.arange(HALF, dtype=jnp.int32) // BS
    diag = (head[:, None] == head[None, :]).astype(jnp.bfloat16)

    def at_far(i, *_):
        chunk = jnp.minimum(i, steps_a - 1)
        return (chunk % half, chunk // half, 0, 0)

    def at_b(i, *_):
        return (jnp.clip(i - steps_a, 0, steps_b - 1), 0)

    def at_far_grad(i, *_):
        return (jnp.clip(i - steps_a - steps_b, 0, steps_a - 1), 0)

    def at_own(i, *_):
        return (jnp.maximum(i - 2 * steps_a - steps_b, 0), 0)

    def at_back(i, *_):
        chunk = jnp.clip(i - steps_a - steps_b, 0, steps_a - 1)
        return (chunk % half, chunk // half, 0, 0)

    def whole(shape):
        return pl.BlockSpec(shape, lambda i, *_: (0,) * len(shape), pipeline_mode=pl.Buffered(1))

    return pl.pallas_call(
        functools.partial(layer_kernel, steps_a, steps_b, far_rows // BS, scaling),
        grid_spec=pltpu.PrefetchScalarGridSpec(
            num_scalar_prefetch=2,
            grid=(steps_a + steps_b + steps_c,),
            in_specs=[
                pl.BlockSpec((per, None, BS, dim), at_far),
                whole((rows, 2 * dim)),
                whole((dim, 2 * dim)),
                pl.BlockSpec((PAIR * BS, dim), at_b),
                pl.BlockSpec((PAIR * BS, dim), at_b),
                whole((HALF, HALF)),
            ],
            out_specs=[
                pl.BlockSpec((PAIR * BS, dim), at_b),
                pl.BlockSpec((PAIR * BS, dim), at_b),
                pl.BlockSpec((ROWS, 2 * dim), at_far_grad),
                pl.BlockSpec((ROWS, 2 * dim), at_own),
                pl.BlockSpec((per, None, BS, dim), at_back),
            ],
            scratch_shapes=[
                pltpu.VMEM((table, BS, dim), jnp.bfloat16),
                pltpu.VMEM((table, BS, dim), jnp.bfloat16),
                pltpu.VMEM((table, BS, dim), jnp.float32),
                pltpu.VMEM((table, BS, dim), jnp.float32),
            ],
        ),
        out_shape=[
            jax.ShapeDtypeStruct((rows, dim), jnp.bfloat16),
            jax.ShapeDtypeStruct((rows, dim), jnp.bfloat16),
            jax.ShapeDtypeStruct((far_rows, 2 * dim), jnp.bfloat16),
            jax.ShapeDtypeStruct((rows, 2 * dim), jnp.bfloat16),
            jax.ShapeDtypeStruct((parts, CAP, BS, dim), jnp.bfloat16),
        ],
        compiler_params=pltpu.CompilerParams(vmem_limit_bytes=60 * 2**20),
    )(entries, counts, far, own_kv, wkv, queries, ups, diag)


def weights_kernel(
    steps_far, core, far_ref, far_grad_ref, own_ref, own_grad_ref, gq_ref, att_ref, cot_ref, mine_ref, give_ref, terms
):
    step = pl.program_id(0)
    rows, dim = own_ref.shape

    @pl.when(step == 0)
    def _():
        own = own_ref[...]
        terms[0] = dot_tn(own, gq_ref[...])
        terms[1] = dot_tn(att_ref[...], cot_ref[...])
        terms[2] = dot_tn(own, own_grad_ref[:, :dim])
        terms[3] = dot_tn(own, own_grad_ref[:, dim:])

    @pl.when(step > 0)
    def _():
        far = far_ref[...].reshape(ROWS, dim)
        terms[2] += dot_tn(far, far_grad_ref[:, :dim])
        terms[3] += dot_tn(far, far_grad_ref[:, dim:])

    @pl.when(step == steps_far)
    def _():
        mine_ref[...] = terms[pl.ds(2 * core[0], 2)]
        give_ref[...] = terms[pl.ds(2 - 2 * core[0], 2)].astype(jnp.bfloat16)


def weights_call(core, far, far_grad, own, own_grad, grad_q, attended, cot):
    rows, dim = own.shape
    steps_far = far_grad.shape[0] // ROWS
    half = steps_far // CAP
    per = ROWS // BS

    def at_far(i, *_):
        chunk = jnp.maximum(i - 1, 0)
        return (chunk % half, chunk // half, 0, 0)

    def whole(shape):
        return pl.BlockSpec(shape, lambda i, *_: (0,) * len(shape), pipeline_mode=pl.Buffered(1))

    return pl.pallas_call(
        functools.partial(weights_kernel, steps_far),
        grid_spec=pltpu.PrefetchScalarGridSpec(
            num_scalar_prefetch=1,
            grid=(steps_far + 1,),
            in_specs=[
                pl.BlockSpec((per, None, BS, dim), at_far),
                pl.BlockSpec((ROWS, 2 * dim), lambda i, *_: (jnp.maximum(i - 1, 0), 0)),
                whole((rows, dim)),
                whole((rows, 2 * dim)),
                whole((rows, dim)),
                whole((rows, dim)),
                whole((rows, dim)),
            ],
            out_specs=[whole((2, dim, dim)), whole((2, dim, dim))],
            scratch_shapes=[pltpu.VMEM((4, dim, dim), jnp.float32)],
        ),
        out_shape=[
            jax.ShapeDtypeStruct((2, dim, dim), jnp.float32),
            jax.ShapeDtypeStruct((2, dim, dim), jnp.bfloat16),
        ],
        compiler_params=pltpu.CompilerParams(vmem_limit_bytes=40 * 2**20),
        cost_estimate=pl.CostEstimate(flops=11 * 10**9, bytes_accessed=20 * 10**6, transcendentals=0),
    )(core, far, far_grad, own, own_grad, grad_q, attended, cot)


def combine_kernel(per, send_ref, base_ref, returned_ref, out_ref, acc):
    step = pl.program_id(0)

    @pl.when(step == 0)
    def _():
        acc[...] = base_ref[...]

    for i in range(per):
        for c in range(CAP):
            acc[send_ref[c, step * per + i]] += returned_ref[i, c].astype(jnp.float32)

    @pl.when(step == pl.num_programs(0) - 1)
    def _():
        out_ref[...] = acc[...].astype(jnp.bfloat16)


def combine_call(send, base, returned):
    blocks, _, dim = base.shape
    parts = returned.shape[0]
    per = 8
    return pl.pallas_call(
        functools.partial(combine_kernel, per),
        grid_spec=pltpu.PrefetchScalarGridSpec(
            num_scalar_prefetch=1,
            grid=(parts // per,),
            in_specs=[
                pl.BlockSpec((blocks, BS, dim), lambda i, *_: (0, 0, 0)),
                pl.BlockSpec((per, CAP, BS, dim), lambda i, *_: (i, 0, 0, 0)),
            ],
            out_specs=pl.BlockSpec((blocks, BS, dim), lambda i, *_: (0, 0, 0)),
            scratch_shapes=[pltpu.VMEM((blocks, BS, dim), jnp.float32)],
        ),
        out_shape=jax.ShapeDtypeStruct((blocks, BS, dim), jnp.bfloat16),
        compiler_params=pltpu.CompilerParams(vmem_limit_bytes=32 * 2**20),
    )(send, base, returned)


def sum_weights(mine, give, nparts, me, returned):
    swap = [(v, v ^ 1) for v in range(nparts)]
    half = mine + lax.ppermute(give, "verts", swap).astype(jnp.float32)
    planes = lax.axis_size("dp")
    here = lax.axis_index("dp")
    rows = half.shape[1] // planes
    total = lax.dynamic_slice_in_dim(half, here * rows, rows, 1)
    for d in range(1, planes):
        there = lax.dynamic_slice_in_dim(half, (here + d) % planes * rows, rows, 1)
        move = [(z, (z + d) % planes) for z in range(planes)]
        total += lax.ppermute(there.astype(jnp.bfloat16), "dp", move).astype(jnp.float32)
    half, returned = lax.optimization_barrier((total, returned))
    side = math.isqrt(nparts // 2)
    wide = nparts // side

    def moved(x, y):
        return [
            (v, y(v // wide) * wide + x(v % wide // 2) * 2 + v % 2) for v in range(nparts)
        ]

    def stay(i):
        return i

    def near(i):
        return i ^ 1

    def wrap(i):
        return side - 1 - i

    in_x = [moved(near, stay), moved(wrap, stay)]
    in_y = [moved(stay, near), moved(stay, wrap)]
    one, two = half[0].astype(jnp.bfloat16), half[1].astype(jnp.bfloat16)
    for here, there in zip(in_x + in_y, in_y + in_x):
        one_other = lax.ppermute(one, "verts", here)
        two_other = lax.ppermute(two, "verts", there)
        last = here is in_y[1]
        one = one.astype(jnp.float32) + one_other.astype(jnp.float32)
        two = two.astype(jnp.float32) + two_other.astype(jnp.float32)
        if not last:
            one, two = one.astype(jnp.bfloat16), two.astype(jnp.bfloat16)
    half = jnp.stack([one, two])
    other = lax.ppermute(half, "verts", swap)
    first = me % 2 == 0
    q_o = jnp.where(first, half, other)
    k_v = jnp.where(first, other, half)
    return jnp.concatenate([q_o[:1], k_v, q_o[1:]], axis=0), returned


def local(feats, weights, grad_out, neighbours, valid):
    nparts = lax.axis_size("verts")
    me = lax.axis_index("verts")
    _, rows, dim = feats.shape
    blocks = rows // BS
    scaling = 1.0 / math.sqrt(dim // H)
    part_ids = jnp.arange(nparts, dtype=jnp.int32)
    inputs_now = feats[0]
    cotangent = grad_out[0]
    w_kv = jnp.concatenate([weights[1], weights[2]], axis=1)

    theirs = neighbours.reshape(nparts, blocks * NNB)
    mine = (theirs // blocks == me) & (part_ids[:, None] != me)
    place = theirs % blocks
    low = jnp.min(jnp.where(mine, place, blocks), axis=1)
    high = jnp.max(jnp.where(mine, place, -1), axis=1)
    send = jnp.stack([low % blocks, jnp.maximum(high, 0)])

    lists = lax.dynamic_slice_in_dim(neighbours, me * blocks, blocks, 0).reshape(-1)
    owner = lists // blocks
    named = owner[:, None] == part_ids[None, :]
    lower = jnp.min(jnp.where(named, (lists % blocks)[:, None], blocks), axis=0)
    slot = (jnp.sum(jnp.where(named, lower[None, :], 0), axis=1) != lists % blocks).astype(jnp.int32)
    entries = jnp.where(owner == me, nparts * CAP + lists % blocks, slot * nparts + owner)
    counts = jnp.sum(valid, axis=1)[lists]

    far = lax.all_to_all(
        inputs_now.reshape(blocks, BS, dim)[send.T.reshape(-1)].reshape(nparts, CAP, BS, dim),
        "verts",
        split_axis=0,
        concat_axis=0,
        tiled=True,
    )

    queries = dot(inputs_now, weights[0]).astype(jnp.bfloat16)
    ups = dot_nt(cotangent, weights[3]).astype(jnp.bfloat16)
    own_kv = dot(inputs_now, w_kv).astype(jnp.bfloat16)

    attended, grad_q, far_grad, own_grad, back = layer_call(
        entries, counts, far, own_kv, w_kv, queries, ups, scaling
    )
    returned = lax.all_to_all(back, "verts", split_axis=0, concat_axis=0, tiled=True)
    mine, give = weights_call(
        (me % 2).reshape(1), far, far_grad, inputs_now, own_grad, grad_q, attended, cotangent
    )
    grad_weights, returned = sum_weights(mine, give, nparts, me, returned)

    attn_out = dot(attended, weights[3]).astype(jnp.bfloat16)
    base = dot_nt(grad_q, weights[0]) + dot_nt(own_grad, w_kv)
    grad_feats = combine_call(send, base.reshape(blocks, BS, dim), returned)
    return (attn_out[None], grad_feats.reshape(1, rows, dim), grad_weights)


def solution(mesh):
    in_specs = (P("dp", "verts", None), P(), P("dp", "verts", None), P(), P())
    out_specs = (P("dp", "verts", None), P("dp", "verts", None), P(None, "dp", None))
    return jax.shard_map(local, mesh=mesh, in_specs=in_specs, out_specs=out_specs, check_vma=False)
```

```python
import functools
import math

import jax
import jax.numpy as jnp
from jax import lax
from jax.experimental import pallas as pl
from jax.experimental.pallas import tpu as pltpu
from jax.sharding import PartitionSpec as P

H = 8
BS = 64
NNB = 8
CAP = 2

ROWS = 1024
PAIR = 4
HALF = 256

NT = (((1,), (1,)), ((), ()))
TN = (((0,), (0,)), ((), ()))


def dot(a, b):
    return jnp.dot(a, b, preferred_element_type=jnp.float32)


def dot_nt(a, b):
    return lax.dot_general(a, b, NT, preferred_element_type=jnp.float32)


def dot_tn(a, b):
    return lax.dot_general(a, b, TN, preferred_element_type=jnp.float32)


def layer_kernel(
    scaling,
    entries,
    counts,
    far_hbm,
    own_k_hbm,
    own_v_hbm,
    wkv_hbm,
    q_hbm,
    u_hbm,
    diag_ref,
    att_hbm,
    gq_hbm,
    gk_hbm,
    gv_hbm,
    back_hbm,
    far_ref,
    wkv_ref,
    q_ref,
    u_ref,
    att_ref,
    gq_ref,
    keys,
    values,
    gkeys,
    gvalues,
    far_sem,
    in_sem,
    out_sem,
    grad_sem,
):
    parts = far_hbm.shape[0]
    remote = parts * CAP
    table, _, dim = keys.shape
    own = table - remote
    per = ROWS // BS
    half_parts = parts // per
    chunks = remote // per

    def far_copy(i):
        lanes = far_hbm.at[pl.ds(i % half_parts * per, per), i // half_parts]
        return pltpu.make_async_copy(lanes, far_ref.at[pl.ds(i * per, per)], far_sem.at[i])

    def back_copy(i):
        lanes = back_hbm.at[pl.ds(i % half_parts * per, per), i // half_parts]
        return pltpu.make_async_copy(far_ref.at[pl.ds(i * per, per)], lanes, far_sem.at[i])

    def grad_copies(first, count, i):
        at = pl.ds(first, count)
        return [
            pltpu.make_async_copy(keys.at[at], gk_hbm.at[at], grad_sem.at[0, i]),
            pltpu.make_async_copy(values.at[at], gv_hbm.at[at], grad_sem.at[1, i]),
        ]

    arrive = [
        pltpu.make_async_copy(wkv_hbm, wkv_ref, in_sem.at[0]),
        pltpu.make_async_copy(own_k_hbm, keys.at[pl.ds(remote, own)], in_sem.at[1]),
        pltpu.make_async_copy(own_v_hbm, values.at[pl.ds(remote, own)], in_sem.at[2]),
        pltpu.make_async_copy(q_hbm, q_ref, in_sem.at[3]),
        pltpu.make_async_copy(u_hbm, u_ref, in_sem.at[4]),
    ]
    arrive[0].start()
    for i in range(chunks):
        far_copy(i).start()
    for copy in arrive[1:]:
        copy.start()
    gkeys[pl.ds(remote, own)] = jnp.zeros((own, BS, dim), jnp.float32)
    gvalues[pl.ds(remote, own)] = jnp.zeros((own, BS, dim), jnp.float32)
    arrive[0].wait()
    for i in range(chunks):
        first = pl.ds(i * per, per)
        far_copy(i).wait()
        both = dot(far_ref[first].reshape(ROWS, dim), wkv_ref[...]).astype(jnp.bfloat16)
        keys[first] = both[:, :dim].reshape(per, BS, dim)
        values[first] = both[:, dim:].reshape(per, BS, dim)
        gkeys[first] = jnp.zeros((per, BS, dim), jnp.float32)
        gvalues[first] = jnp.zeros((per, BS, dim), jnp.float32)
    for copy in arrive[1:]:
        copy.wait()

    place = lax.broadcasted_iota(jnp.int32, (BS, HALF), 0)
    lane_head = lax.broadcasted_iota(jnp.int32, (BS, HALF), 1) // BS

    def attend(step, carry):
        diag = diag_ref[...]

        def first_half(sub, half):
            at = pl.ds(pl.multiple_of((step * PAIR + sub) * BS, BS), BS)
            cols = slice(half * HALF, (half + 1) * HALF)
            base = (step * PAIR + sub) * NNB
            ids = [entries[base + n] for n in range(NNB)]
            ends = [counts[base + n] for n in range(NNB)]
            queries = q_ref[at, cols] * jnp.bfloat16(scaling)
            qbd = jnp.concatenate([queries] * (HALF // BS), axis=0) * diag
            ubd = jnp.concatenate([u_ref[at, cols]] * (HALF // BS), axis=0) * diag
            k_all = jnp.concatenate([keys[i, :, cols] for i in ids], axis=0)
            v_all = jnp.concatenate([values[i, :, cols] for i in ids], axis=0)
            return at, cols, ids, ends, qbd, ubd, k_all, v_all, dot_nt(k_all, qbd), dot_nt(v_all, ubd)

        def second_half(at, cols, ids, ends, qbd, ubd, k_all, v_all, scores, dprob):
            scores = jnp.concatenate(
                [
                    jnp.where(place < ends[n], scores[n * BS : (n + 1) * BS], -1e30)
                    for n in range(NNB)
                ],
                axis=0,
            )
            top = jnp.max(scores, axis=0, keepdims=True)
            raised = jnp.exp(scores - top)
            probs = raised * (1.0 / jnp.sum(raised, axis=0, keepdims=True))
            probs_b = probs.astype(jnp.bfloat16)
            inner = jnp.sum(probs * dprob, axis=0, keepdims=True)
            dscore = (probs * (dprob - inner)).astype(jnp.bfloat16)
            grad_v = dot(probs_b, ubd)
            grad_k = dot(dscore, qbd)
            att_wide = dot_tn(probs_b, v_all)
            gq_wide = dot_tn(dscore, k_all)
            att = att_wide[:BS]
            gq = gq_wide[:BS]
            for h in range(1, HALF // BS):
                rows = slice(h * BS, (h + 1) * BS)
                att = jnp.where(lane_head == h, att_wide[rows], att)
                gq = jnp.where(lane_head == h, gq_wide[rows], gq)
            att_ref[at, cols] = att.astype(jnp.bfloat16)
            gq_ref[at, cols] = (gq * scaling).astype(jnp.bfloat16)
            for n in range(NNB):
                rows = slice(n * BS, (n + 1) * BS)
                gkeys[ids[n], :, cols] += grad_k[rows]
                gvalues[ids[n], :, cols] += grad_v[rows]

        todo = [(sub, half) for sub in range(PAIR) for half in range(dim // HALF)]
        held = first_half(*todo[0])
        for after in todo[1:] + [None]:
            ahead = first_half(*after) if after else None
            second_half(*held)
            held = ahead
        return carry

    lax.fori_loop(0, own // PAIR, attend, 0)

    leave = [
        pltpu.make_async_copy(att_ref, att_hbm, out_sem.at[0]),
        pltpu.make_async_copy(gq_ref, gq_hbm, out_sem.at[1]),
    ]
    last = pl.ds(remote, own)
    keys[last] = gkeys[last].astype(jnp.bfloat16)
    values[last] = gvalues[last].astype(jnp.bfloat16)
    leave += grad_copies(remote, own, chunks)
    for copy in leave:
        copy.start()
    for i in range(chunks):
        first = pl.ds(i * per, per)
        grad_k = gkeys[first].astype(jnp.bfloat16)
        grad_v = gvalues[first].astype(jnp.bfloat16)
        keys[first] = grad_k
        values[first] = grad_v
        grads = grad_copies(i * per, per, i)
        for copy in grads:
            copy.start()
        back = dot_nt(grad_k.reshape(ROWS, dim), wkv_ref[:, :dim]) + dot_nt(
            grad_v.reshape(ROWS, dim), wkv_ref[:, dim:]
        )
        far_ref[first] = back.astype(jnp.bfloat16).reshape(per, BS, dim)
        back_copy(i).start()
        leave += grads + [back_copy(i)]
    for copy in leave:
        copy.wait()


def layer_call(entries, counts, far, own_k, own_v, wkv, queries, ups, scaling):
    parts, _, _, dim = far.shape
    rows = queries.shape[0]
    own = rows // BS
    table = parts * CAP + own
    chunks = parts * CAP * BS // ROWS
    head = jnp.arange(HALF, dtype=jnp.int32) // BS
    diag = (head[:, None] == head[None, :]).astype(jnp.bfloat16)
    anywhere = pl.BlockSpec(memory_space=pl.ANY)
    return pl.pallas_call(
        functools.partial(layer_kernel, scaling),
        grid_spec=pltpu.PrefetchScalarGridSpec(
            num_scalar_prefetch=2,
            grid=(1,),
            in_specs=[anywhere] * 6 + [pl.BlockSpec((HALF, HALF), lambda i, *_: (0, 0))],
            out_specs=[anywhere] * 5,
            scratch_shapes=[
                pltpu.VMEM((parts * CAP, BS, dim), jnp.bfloat16),
                pltpu.VMEM((dim, 2 * dim), jnp.bfloat16),
                pltpu.VMEM((rows, dim), jnp.bfloat16),
                pltpu.VMEM((rows, dim), jnp.bfloat16),
                pltpu.VMEM((rows, dim), jnp.bfloat16),
                pltpu.VMEM((rows, dim), jnp.bfloat16),
                pltpu.VMEM((table, BS, dim), jnp.bfloat16),
                pltpu.VMEM((table, BS, dim), jnp.bfloat16),
                pltpu.VMEM((table, BS, dim), jnp.float32),
                pltpu.VMEM((table, BS, dim), jnp.float32),
                pltpu.SemaphoreType.DMA((chunks,)),
                pltpu.SemaphoreType.DMA((5,)),
                pltpu.SemaphoreType.DMA((2,)),
                pltpu.SemaphoreType.DMA((2, chunks + 1)),
            ],
        ),
        out_shape=[
            jax.ShapeDtypeStruct((rows, dim), jnp.bfloat16),
            jax.ShapeDtypeStruct((rows, dim), jnp.bfloat16),
            jax.ShapeDtypeStruct((table, BS, dim), jnp.bfloat16),
            jax.ShapeDtypeStruct((table, BS, dim), jnp.bfloat16),
            jax.ShapeDtypeStruct(far.shape, jnp.bfloat16),
        ],
        compiler_params=pltpu.CompilerParams(vmem_limit_bytes=60 * 2**20),
    )(entries, counts, far, own_k, own_v, wkv, queries, ups, diag)


def weights_kernel(
    steps_far, core, far_ref, gk_ref, gv_ref, own_ref, gq_ref, att_ref, cot_ref, mine_ref, give_ref, terms
):
    step = pl.program_id(0)
    rows, dim = own_ref.shape
    grad_k = gk_ref[...].reshape(ROWS, dim)
    grad_v = gv_ref[...].reshape(ROWS, dim)

    @pl.when(step < steps_far)
    def _():
        far = far_ref[...].reshape(ROWS, dim)
        from_k = dot_tn(far, grad_k)
        from_v = dot_tn(far, grad_v)

        @pl.when(step == 0)
        def _():
            terms[2] = from_k
            terms[3] = from_v

        @pl.when(step > 0)
        def _():
            terms[2] += from_k
            terms[3] += from_v

    @pl.when(step == steps_far)
    def _():
        own = own_ref[...]
        terms[0] = dot_tn(own, gq_ref[...])
        terms[1] = dot_tn(att_ref[...], cot_ref[...])
        terms[2] += dot_tn(own, grad_k)
        terms[3] += dot_tn(own, grad_v)
        mine_ref[...] = terms[pl.ds(2 * core[0], 2)]
        give_ref[...] = terms[pl.ds(2 - 2 * core[0], 2)].astype(jnp.bfloat16)


def weights_call(core, far, grad_k, grad_v, own, grad_q, attended, cot):
    rows, dim = own.shape
    steps_far = far.shape[0] * CAP * BS // ROWS
    half = steps_far // CAP
    per = ROWS // BS

    def at_far(i, *_):
        chunk = jnp.minimum(i, steps_far - 1)
        return (chunk % half, chunk // half, 0, 0)

    def whole(shape):
        return pl.BlockSpec(shape, lambda i, *_: (0,) * len(shape), pipeline_mode=pl.Buffered(1))

    return pl.pallas_call(
        functools.partial(weights_kernel, steps_far),
        grid_spec=pltpu.PrefetchScalarGridSpec(
            num_scalar_prefetch=1,
            grid=(steps_far + 1,),
            in_specs=[
                pl.BlockSpec((per, None, BS, dim), at_far),
                pl.BlockSpec((per, BS, dim), lambda i, *_: (i, 0, 0)),
                pl.BlockSpec((per, BS, dim), lambda i, *_: (i, 0, 0)),
                whole((rows, dim)),
                whole((rows, dim)),
                whole((rows, dim)),
                whole((rows, dim)),
            ],
            out_specs=[whole((2, dim, dim)), whole((2, dim, dim))],
            scratch_shapes=[pltpu.VMEM((4, dim, dim), jnp.float32)],
        ),
        out_shape=[
            jax.ShapeDtypeStruct((2, dim, dim), jnp.float32),
            jax.ShapeDtypeStruct((2, dim, dim), jnp.bfloat16),
        ],
        compiler_params=pltpu.CompilerParams(vmem_limit_bytes=60 * 2**20),
        cost_estimate=pl.CostEstimate(flops=11 * 10**9, bytes_accessed=20 * 10**6, transcendentals=0),
    )(core, far, grad_k, grad_v, own, grad_q, attended, cot)


def combine_kernel(per, send_ref, base_ref, returned_ref, out_ref, acc):
    step = pl.program_id(0)

    @pl.when(step == 0)
    def _():
        acc[...] = base_ref[...]

    for i in range(per):
        for c in range(CAP):
            acc[send_ref[c, step * per + i]] += returned_ref[i, c].astype(jnp.float32)

    @pl.when(step == pl.num_programs(0) - 1)
    def _():
        out_ref[...] = acc[...].astype(jnp.bfloat16)


def combine_call(send, base, returned):
    blocks, _, dim = base.shape
    parts = returned.shape[0]
    per = 8
    return pl.pallas_call(
        functools.partial(combine_kernel, per),
        grid_spec=pltpu.PrefetchScalarGridSpec(
            num_scalar_prefetch=1,
            grid=(parts // per,),
            in_specs=[
                pl.BlockSpec((blocks, BS, dim), lambda i, *_: (0, 0, 0)),
                pl.BlockSpec((per, CAP, BS, dim), lambda i, *_: (i, 0, 0, 0)),
            ],
            out_specs=pl.BlockSpec((blocks, BS, dim), lambda i, *_: (0, 0, 0)),
            scratch_shapes=[pltpu.VMEM((blocks, BS, dim), jnp.float32)],
        ),
        out_shape=jax.ShapeDtypeStruct((blocks, BS, dim), jnp.bfloat16),
        compiler_params=pltpu.CompilerParams(vmem_limit_bytes=32 * 2**20),
    )(send, base, returned)


def sum_weights(mine, give, nparts, me, returned):
    swap = [(v, v ^ 1) for v in range(nparts)]
    half = mine + lax.ppermute(give, "verts", swap).astype(jnp.float32)
    planes = lax.axis_size("dp")
    here = lax.axis_index("dp")
    rows = half.shape[1] // planes
    total = lax.dynamic_slice_in_dim(half, here * rows, rows, 1)
    for d in range(1, planes):
        there = lax.dynamic_slice_in_dim(half, (here + d) % planes * rows, rows, 1)
        move = [(z, (z + d) % planes) for z in range(planes)]
        total += lax.ppermute(there.astype(jnp.bfloat16), "dp", move).astype(jnp.float32)
    half = total
    side = math.isqrt(nparts // 2)
    wide = nparts // side

    def moved(x, y):
        return [
            (v, y(v // wide) * wide + x(v % wide // 2) * 2 + v % 2) for v in range(nparts)
        ]

    def stay(i):
        return i

    def near(i):
        return i ^ 1

    def wrap(i):
        return side - 1 - i

    in_x = [moved(near, stay), moved(wrap, stay)]
    in_y = [moved(stay, near), moved(stay, wrap)]
    one, two = half[0].astype(jnp.bfloat16), half[1].astype(jnp.bfloat16)
    for here, there in zip(in_x + in_y, in_y + in_x):
        one_other = lax.ppermute(one, "verts", here)
        two_other = lax.ppermute(two, "verts", there)
        if here is in_x[0]:
            one_other, two_other, returned = lax.optimization_barrier((one_other, two_other, returned))
        last = here is in_y[1]
        one = one.astype(jnp.float32) + one_other.astype(jnp.float32)
        two = two.astype(jnp.float32) + two_other.astype(jnp.float32)
        if not last:
            one, two = one.astype(jnp.bfloat16), two.astype(jnp.bfloat16)
    half = jnp.stack([one, two])
    other = lax.ppermute(half, "verts", swap)
    first = me % 2 == 0
    q_o = jnp.where(first, half, other)
    k_v = jnp.where(first, other, half)
    return jnp.concatenate([q_o[:1], k_v, q_o[1:]], axis=0), returned


def local(feats, weights, grad_out, neighbours, valid):
    nparts = lax.axis_size("verts")
    me = lax.axis_index("verts")
    _, rows, dim = feats.shape
    blocks = rows // BS
    scaling = 1.0 / math.sqrt(dim // H)
    part_ids = jnp.arange(nparts, dtype=jnp.int32)
    inputs_now = feats[0]
    cotangent = grad_out[0]
    w_kv = jnp.concatenate([weights[1], weights[2]], axis=1)

    theirs = neighbours.reshape(nparts, blocks * NNB)
    mine = (theirs // blocks == me) & (part_ids[:, None] != me)
    place = theirs % blocks
    low = jnp.min(jnp.where(mine, place, blocks), axis=1)
    high = jnp.max(jnp.where(mine, place, -1), axis=1)
    send = jnp.stack([low % blocks, jnp.maximum(high, 0)])

    lists = lax.dynamic_slice_in_dim(neighbours, me * blocks, blocks, 0).reshape(-1)
    owner = lists // blocks
    named = owner[:, None] == part_ids[None, :]
    lower = jnp.min(jnp.where(named, (lists % blocks)[:, None], blocks), axis=0)
    slot = (jnp.sum(jnp.where(named, lower[None, :], 0), axis=1) != lists % blocks).astype(jnp.int32)
    entries = jnp.where(owner == me, nparts * CAP + lists % blocks, slot * nparts + owner)
    counts = jnp.sum(valid, axis=1)[lists]

    far = lax.all_to_all(
        inputs_now.reshape(blocks, BS, dim)[send.T.reshape(-1)].reshape(nparts, CAP, BS, dim),
        "verts",
        split_axis=0,
        concat_axis=0,
        tiled=True,
    )

    queries = dot(inputs_now, weights[0]).astype(jnp.bfloat16)
    ups = dot_nt(cotangent, weights[3]).astype(jnp.bfloat16)
    own_k = dot(inputs_now, weights[1]).astype(jnp.bfloat16).reshape(blocks, BS, dim)
    own_v = dot(inputs_now, weights[2]).astype(jnp.bfloat16).reshape(blocks, BS, dim)

    attended, grad_q, grad_k, grad_v, back = layer_call(
        entries, counts, far, own_k, own_v, w_kv, queries, ups, scaling
    )
    returned = lax.all_to_all(back, "verts", split_axis=0, concat_axis=0, tiled=True)
    mine, give = weights_call(
        (me % 2).reshape(1), far, grad_k, grad_v, inputs_now, grad_q, attended, cotangent
    )
    grad_weights, returned = sum_weights(mine, give, nparts, me, returned)

    attn_out = dot(attended, weights[3]).astype(jnp.bfloat16)
    own_gk = grad_k[nparts * CAP :].reshape(rows, dim)
    own_gv = grad_v[nparts * CAP :].reshape(rows, dim)
    base = dot_nt(grad_q, weights[0]) + dot_nt(own_gk, weights[1]) + dot_nt(own_gv, weights[2])
    grad_feats = combine_call(send, base.reshape(blocks, BS, dim), returned)
    return (attn_out[None], grad_feats.reshape(1, rows, dim), grad_weights)


def solution(mesh):
    in_specs = (P("dp", "verts", None), P(), P("dp", "verts", None), P(), P())
    out_specs = (P("dp", "verts", None), P("dp", "verts", None), P(None, "dp", None))
    return jax.shard_map(local, mesh=mesh, in_specs=in_specs, out_specs=out_specs, check_vma=False)
```

```python
import functools
import math

import jax
import jax.numpy as jnp
from jax import lax
from jax.experimental import pallas as pl
from jax.experimental.pallas import tpu as pltpu
from jax.sharding import PartitionSpec as P

H = 8
BS = 64
NNB = 8
CAP = 2

ROWS = 1024
PAIR = 16
HALF = 256

NT = (((1,), (1,)), ((), ()))
TN = (((0,), (0,)), ((), ()))


def dot(a, b):
    return jnp.dot(a, b, preferred_element_type=jnp.float32)


def dot_nt(a, b):
    return lax.dot_general(a, b, NT, preferred_element_type=jnp.float32)


def dot_tn(a, b):
    return lax.dot_general(a, b, TN, preferred_element_type=jnp.float32)


def layer_kernel(
    scaling,
    entries,
    counts,
    far_hbm,
    own_k_hbm,
    own_v_hbm,
    wkv_hbm,
    q_hbm,
    u_hbm,
    diag_ref,
    att_hbm,
    gq_hbm,
    gk_hbm,
    gv_hbm,
    own_gk_hbm,
    own_gv_hbm,
    back_hbm,
    far_ref,
    wkv_ref,
    q_ref,
    u_ref,
    att_ref,
    gq_ref,
    keys,
    values,
    gkeys,
    gvalues,
    far_sem,
    in_sem,
    out_sem,
    grad_sem,
):
    parts = far_hbm.shape[0]
    remote = parts * CAP
    table, _, dim = keys.shape
    own = table - remote
    per = ROWS // BS
    half_parts = parts // per
    chunks = remote // per

    def far_copy(i):
        lanes = far_hbm.at[pl.ds(i % half_parts * per, per), i // half_parts]
        return pltpu.make_async_copy(lanes, far_ref.at[pl.ds(i * per, per)], far_sem.at[i])

    def back_copy(i):
        lanes = back_hbm.at[pl.ds(i % half_parts * per, per), i // half_parts]
        return pltpu.make_async_copy(far_ref.at[pl.ds(i * per, per)], lanes, far_sem.at[i])

    def grad_copies(i):
        at = pl.ds(i * per, per)
        return [
            pltpu.make_async_copy(keys.at[at], gk_hbm.at[at], grad_sem.at[0, i]),
            pltpu.make_async_copy(values.at[at], gv_hbm.at[at], grad_sem.at[1, i]),
        ]

    arrive = [
        pltpu.make_async_copy(wkv_hbm, wkv_ref, in_sem.at[0]),
        pltpu.make_async_copy(own_k_hbm, keys.at[pl.ds(remote, own)], in_sem.at[1]),
        pltpu.make_async_copy(own_v_hbm, values.at[pl.ds(remote, own)], in_sem.at[2]),
        pltpu.make_async_copy(q_hbm, q_ref, in_sem.at[3]),
        pltpu.make_async_copy(u_hbm, u_ref, in_sem.at[4]),
    ]
    arrive[0].start()
    for i in range(chunks):
        far_copy(i).start()
    for copy in arrive[1:]:
        copy.start()
    gkeys[pl.ds(remote, own)] = jnp.zeros((own, BS, dim), jnp.float32)
    gvalues[pl.ds(remote, own)] = jnp.zeros((own, BS, dim), jnp.float32)
    arrive[0].wait()
    for i in range(chunks):
        first = pl.ds(i * per, per)
        far_copy(i).wait()
        both = dot(far_ref[first].reshape(ROWS, dim), wkv_ref[...]).astype(jnp.bfloat16)
        keys[first] = both[:, :dim].reshape(per, BS, dim)
        values[first] = both[:, dim:].reshape(per, BS, dim)
        gkeys[first] = jnp.zeros((per, BS, dim), jnp.float32)
        gvalues[first] = jnp.zeros((per, BS, dim), jnp.float32)
    for copy in arrive[1:]:
        copy.wait()

    place = lax.broadcasted_iota(jnp.int32, (BS, HALF), 0)
    lane_head = lax.broadcasted_iota(jnp.int32, (BS, HALF), 1) // BS

    def attend(step, carry):
        diag = diag_ref[...]

        def first_half(sub, half):
            at = pl.ds(pl.multiple_of((step * PAIR + sub) * BS, BS), BS)
            cols = slice(half * HALF, (half + 1) * HALF)
            base = (step * PAIR + sub) * NNB
            ids = [entries[base + n] for n in range(NNB)]
            ends = [counts[base + n] for n in range(NNB)]
            queries = q_ref[at, cols] * jnp.bfloat16(scaling)
            qbd = jnp.concatenate([queries] * (HALF // BS), axis=0) * diag
            ubd = jnp.concatenate([u_ref[at, cols]] * (HALF // BS), axis=0) * diag
            k_all = jnp.concatenate([keys[i, :, cols] for i in ids], axis=0)
            v_all = jnp.concatenate([values[i, :, cols] for i in ids], axis=0)
            return at, cols, ids, ends, qbd, ubd, k_all, v_all, dot_nt(k_all, qbd), dot_nt(v_all, ubd)

        def second_half(at, cols, ids, ends, qbd, ubd, k_all, v_all, scores, dprob):
            scores = jnp.concatenate(
                [
                    jnp.where(place < ends[n], scores[n * BS : (n + 1) * BS], -1e30)
                    for n in range(NNB)
                ],
                axis=0,
            )
            top = jnp.max(scores, axis=0, keepdims=True)
            raised = jnp.exp(scores - top)
            probs = raised * (1.0 / jnp.sum(raised, axis=0, keepdims=True))
            probs_b = probs.astype(jnp.bfloat16)
            inner = jnp.sum(probs * dprob, axis=0, keepdims=True)
            dscore = (probs * (dprob - inner)).astype(jnp.bfloat16)
            grad_v = dot(probs_b, ubd)
            grad_k = dot(dscore, qbd)
            att_wide = dot_tn(probs_b, v_all)
            gq_wide = dot_tn(dscore, k_all)
            att = att_wide[:BS]
            gq = gq_wide[:BS]
            for h in range(1, HALF // BS):
                rows = slice(h * BS, (h + 1) * BS)
                att = jnp.where(lane_head == h, att_wide[rows], att)
                gq = jnp.where(lane_head == h, gq_wide[rows], gq)
            att_ref[at, cols] = att.astype(jnp.bfloat16)
            gq_ref[at, cols] = (gq * scaling).astype(jnp.bfloat16)
            for n in range(NNB):
                rows = slice(n * BS, (n + 1) * BS)
                gkeys[ids[n], :, cols] += grad_k[rows]
                gvalues[ids[n], :, cols] += grad_v[rows]

        todo = [(sub, half) for sub in range(PAIR) for half in range(dim // HALF)]
        held = first_half(*todo[0])
        for after in todo[1:] + [None]:
            ahead = first_half(*after) if after else None
            second_half(*held)
            held = ahead
        return carry

    lax.fori_loop(0, own // PAIR, attend, 0)

    leave = [
        pltpu.make_async_copy(att_ref, att_hbm, out_sem.at[0]),
        pltpu.make_async_copy(gq_ref, gq_hbm, out_sem.at[1]),
    ]
    last = pl.ds(remote, own)
    keys[last] = gkeys[last].astype(jnp.bfloat16)
    values[last] = gvalues[last].astype(jnp.bfloat16)
    leave += [
        pltpu.make_async_copy(keys.at[last], own_gk_hbm, out_sem.at[2]),
        pltpu.make_async_copy(values.at[last], own_gv_hbm, out_sem.at[3]),
    ]
    for copy in leave:
        copy.start()
    for i in range(chunks):
        first = pl.ds(i * per, per)
        grad_k = gkeys[first].astype(jnp.bfloat16)
        grad_v = gvalues[first].astype(jnp.bfloat16)
        keys[first] = grad_k
        values[first] = grad_v
        grads = grad_copies(i)
        for copy in grads:
            copy.start()
        back = dot_nt(grad_k.reshape(ROWS, dim), wkv_ref[:, :dim]) + dot_nt(
            grad_v.reshape(ROWS, dim), wkv_ref[:, dim:]
        )
        far_ref[first] = back.astype(jnp.bfloat16).reshape(per, BS, dim)
        back_copy(i).start()
        leave += grads + [back_copy(i)]
    for copy in leave:
        copy.wait()


def layer_call(entries, counts, far, own_k, own_v, wkv, queries, ups, scaling):
    parts, _, _, dim = far.shape
    rows = queries.shape[0]
    own = rows // BS
    table = parts * CAP + own
    chunks = parts * CAP * BS // ROWS
    head = jnp.arange(HALF, dtype=jnp.int32) // BS
    diag = (head[:, None] == head[None, :]).astype(jnp.bfloat16)
    anywhere = pl.BlockSpec(memory_space=pl.ANY)
    return pl.pallas_call(
        functools.partial(layer_kernel, scaling),
        grid_spec=pltpu.PrefetchScalarGridSpec(
            num_scalar_prefetch=2,
            grid=(1,),
            in_specs=[anywhere] * 6 + [pl.BlockSpec((HALF, HALF), lambda i, *_: (0, 0))],
            out_specs=[anywhere] * 7,
            scratch_shapes=[
                pltpu.VMEM((parts * CAP, BS, dim), jnp.bfloat16),
                pltpu.VMEM((dim, 2 * dim), jnp.bfloat16),
                pltpu.VMEM((rows, dim), jnp.bfloat16),
                pltpu.VMEM((rows, dim), jnp.bfloat16),
                pltpu.VMEM((rows, dim), jnp.bfloat16),
                pltpu.VMEM((rows, dim), jnp.bfloat16),
                pltpu.VMEM((table, BS, dim), jnp.bfloat16),
                pltpu.VMEM((table, BS, dim), jnp.bfloat16),
                pltpu.VMEM((table, BS, dim), jnp.float32),
                pltpu.VMEM((table, BS, dim), jnp.float32),
                pltpu.SemaphoreType.DMA((chunks,)),
                pltpu.SemaphoreType.DMA((5,)),
                pltpu.SemaphoreType.DMA((4,)),
                pltpu.SemaphoreType.DMA((2, chunks)),
            ],
        ),
        out_shape=[
            jax.ShapeDtypeStruct((rows, dim), jnp.bfloat16),
            jax.ShapeDtypeStruct((rows, dim), jnp.bfloat16),
            jax.ShapeDtypeStruct((parts * CAP, BS, dim), jnp.bfloat16),
            jax.ShapeDtypeStruct((parts * CAP, BS, dim), jnp.bfloat16),
            jax.ShapeDtypeStruct((own, BS, dim), jnp.bfloat16),
            jax.ShapeDtypeStruct((own, BS, dim), jnp.bfloat16),
            jax.ShapeDtypeStruct(far.shape, jnp.bfloat16),
        ],
        compiler_params=pltpu.CompilerParams(vmem_limit_bytes=60 * 2**20),
    )(entries, counts, far, own_k, own_v, wkv, queries, ups, diag)


def weights_kernel(
    steps_far, core, far_ref, gk_ref, gv_ref, own_gk_ref, own_gv_ref, own_ref, gq_ref, att_ref, cot_ref, mine_ref, give_ref, terms
):
    step = pl.program_id(0)
    rows, dim = own_ref.shape

    @pl.when(step < steps_far)
    def _():
        far = far_ref[...].reshape(ROWS, dim)
        from_k = dot_tn(far, gk_ref[...].reshape(ROWS, dim))
        from_v = dot_tn(far, gv_ref[...].reshape(ROWS, dim))

        @pl.when(step == 0)
        def _():
            terms[2] = from_k
            terms[3] = from_v

        @pl.when(step > 0)
        def _():
            terms[2] += from_k
            terms[3] += from_v

    @pl.when(step == steps_far)
    def _():
        own = own_ref[...]
        terms[0] = dot_tn(own, gq_ref[...])
        terms[1] = dot_tn(att_ref[...], cot_ref[...])
        terms[2] += dot_tn(own, own_gk_ref[...])
        terms[3] += dot_tn(own, own_gv_ref[...])
        mine_ref[...] = terms[pl.ds(2 * core[0], 2)]
        give_ref[...] = terms[pl.ds(2 - 2 * core[0], 2)].astype(jnp.bfloat16)


def weights_call(core, far, grad_k, grad_v, own_gk, own_gv, own, grad_q, attended, cot):
    rows, dim = own.shape
    steps_far = far.shape[0] * CAP * BS // ROWS
    half = steps_far // CAP
    per = ROWS // BS

    def at_far(i, *_):
        chunk = jnp.minimum(i, steps_far - 1)
        return (chunk % half, chunk // half, 0, 0)

    def whole(shape):
        return pl.BlockSpec(shape, lambda i, *_: (0,) * len(shape), pipeline_mode=pl.Buffered(1))

    return pl.pallas_call(
        functools.partial(weights_kernel, steps_far),
        grid_spec=pltpu.PrefetchScalarGridSpec(
            num_scalar_prefetch=1,
            grid=(steps_far + 1,),
            in_specs=[
                pl.BlockSpec((per, None, BS, dim), at_far),
                pl.BlockSpec((per, BS, dim), lambda i, *_: (jnp.minimum(i, steps_far - 1), 0, 0)),
                pl.BlockSpec((per, BS, dim), lambda i, *_: (jnp.minimum(i, steps_far - 1), 0, 0)),
                whole((rows, dim)),
                whole((rows, dim)),
                whole((rows, dim)),
                whole((rows, dim)),
                whole((rows, dim)),
                whole((rows, dim)),
            ],
            out_specs=[whole((2, dim, dim)), whole((2, dim, dim))],
            scratch_shapes=[pltpu.VMEM((4, dim, dim), jnp.float32)],
        ),
        out_shape=[
            jax.ShapeDtypeStruct((2, dim, dim), jnp.float32),
            jax.ShapeDtypeStruct((2, dim, dim), jnp.bfloat16),
        ],
        compiler_params=pltpu.CompilerParams(vmem_limit_bytes=60 * 2**20),
        cost_estimate=pl.CostEstimate(flops=11 * 10**9, bytes_accessed=20 * 10**6, transcendentals=0),
    )(core, far, grad_k, grad_v, own_gk, own_gv, own, grad_q, attended, cot)


def combine_kernel(per, send_ref, base_ref, returned_ref, out_ref, acc):
    step = pl.program_id(0)

    @pl.when(step == 0)
    def _():
        acc[...] = base_ref[...]

    for i in range(per):
        for c in range(CAP):
            acc[send_ref[c, step * per + i]] += returned_ref[i, c].astype(jnp.float32)

    @pl.when(step == pl.num_programs(0) - 1)
    def _():
        out_ref[...] = acc[...].astype(jnp.bfloat16)


def combine_call(send, base, returned):
    blocks, _, dim = base.shape
    parts = returned.shape[0]
    per = 8
    return pl.pallas_call(
        functools.partial(combine_kernel, per),
        grid_spec=pltpu.PrefetchScalarGridSpec(
            num_scalar_prefetch=1,
            grid=(parts // per,),
            in_specs=[
                pl.BlockSpec((blocks, BS, dim), lambda i, *_: (0, 0, 0)),
                pl.BlockSpec((per, CAP, BS, dim), lambda i, *_: (i, 0, 0, 0)),
            ],
            out_specs=pl.BlockSpec((blocks, BS, dim), lambda i, *_: (0, 0, 0)),
            scratch_shapes=[pltpu.VMEM((blocks, BS, dim), jnp.float32)],
        ),
        out_shape=jax.ShapeDtypeStruct((blocks, BS, dim), jnp.bfloat16),
        compiler_params=pltpu.CompilerParams(vmem_limit_bytes=32 * 2**20),
    )(send, base, returned)


def over_cores_and_planes(mine, give, nparts):
    half = mine + lax.ppermute(give, "verts", [(v, v ^ 1) for v in range(nparts)]).astype(jnp.float32)
    planes = lax.axis_size("dp")
    here = lax.axis_index("dp")
    rows = half.shape[1] // planes
    total = lax.dynamic_slice_in_dim(half, here * rows, rows, 1)
    for d in range(1, planes):
        there = lax.dynamic_slice_in_dim(half, (here + d) % planes * rows, rows, 1)
        move = [(z, (z + d) % planes) for z in range(planes)]
        total += lax.ppermute(there.astype(jnp.bfloat16), "dp", move).astype(jnp.float32)
    return total


def moved(nparts, dx, dy):
    side = math.isqrt(nparts // 2)
    wide = nparts // side

    def go(i, d):
        return d(i) if callable(d) else (i + d) % side

    return [
        (v, go(v // wide, dy) * wide + go(v % wide // 2, dx) * 2 + v % 2) for v in range(nparts)
    ]


def ring_parts(value, nparts, along_x):
    side = math.isqrt(nparts // 2)
    moves = [moved(nparts, d, 0) if along_x else moved(nparts, 0, d) for d in range(1, side)]
    return [lax.ppermute(value, "verts", move) for move in moves]


def ring_sum(value, parts):
    one, two, three = [part.astype(jnp.float32) for part in parts]
    return ((value.astype(jnp.float32) + two) + (one + three)).astype(jnp.bfloat16)


def pair_sum(value, nparts, partner, along_x):
    move = moved(nparts, partner, 0) if along_x else moved(nparts, 0, partner)
    return value.astype(jnp.float32) + lax.ppermute(value, "verts", move).astype(jnp.float32)


def local(feats, weights, grad_out, neighbours, valid):
    nparts = lax.axis_size("verts")
    me = lax.axis_index("verts")
    _, rows, dim = feats.shape
    blocks = rows // BS
    scaling = 1.0 / math.sqrt(dim // H)
    part_ids = jnp.arange(nparts, dtype=jnp.int32)
    inputs_now = feats[0]
    cotangent = grad_out[0]
    w_kv = jnp.concatenate([weights[1], weights[2]], axis=1)

    theirs = neighbours.reshape(nparts, blocks * NNB)
    mine = (theirs // blocks == me) & (part_ids[:, None] != me)
    place = theirs % blocks
    low = jnp.min(jnp.where(mine, place, blocks), axis=1)
    high = jnp.max(jnp.where(mine, place, -1), axis=1)
    send = jnp.stack([low % blocks, jnp.maximum(high, 0)])

    lists = lax.dynamic_slice_in_dim(neighbours, me * blocks, blocks, 0).reshape(-1)
    owner = lists // blocks
    named = owner[:, None] == part_ids[None, :]
    lower = jnp.min(jnp.where(named, (lists % blocks)[:, None], blocks), axis=0)
    slot = (jnp.sum(jnp.where(named, lower[None, :], 0), axis=1) != lists % blocks).astype(jnp.int32)
    entries = jnp.where(owner == me, nparts * CAP + lists % blocks, slot * nparts + owner)
    counts = jnp.sum(valid, axis=1)[lists]

    far = lax.all_to_all(
        inputs_now.reshape(blocks, BS, dim)[send.T.reshape(-1)].reshape(nparts, CAP, BS, dim),
        "verts",
        split_axis=0,
        concat_axis=0,
        tiled=True,
    )

    queries = dot(inputs_now, weights[0]).astype(jnp.bfloat16)
    ups = dot_nt(cotangent, weights[3]).astype(jnp.bfloat16)
    own_k = dot(inputs_now, weights[1]).astype(jnp.bfloat16).reshape(blocks, BS, dim)
    own_v = dot(inputs_now, weights[2]).astype(jnp.bfloat16).reshape(blocks, BS, dim)

    attended, grad_q, grad_k, grad_v, own_gk, own_gv, back = layer_call(
        entries, counts, far, own_k, own_v, w_kv, queries, ups, scaling
    )
    own_gk, own_gv = own_gk.reshape(rows, dim), own_gv.reshape(rows, dim)
    returned = lax.all_to_all(back, "verts", split_axis=0, concat_axis=0, tiled=True)
    mine, give = weights_call(
        (me % 2).reshape(1),
        far,
        grad_k,
        grad_v,
        own_gk,
        own_gv,
        inputs_now,
        grad_q,
        attended,
        cotangent,
    )
    total = over_cores_and_planes(mine, give, nparts)
    attn_out = dot(attended, weights[3]).astype(jnp.bfloat16)
    base = dot_nt(grad_q, weights[0]) + dot_nt(own_gk, weights[1]) + dot_nt(own_gv, weights[2])
    total, attn_out, base = lax.optimization_barrier((total, attn_out, base))

    side = math.isqrt(nparts // 2)
    one, two = total[0].astype(jnp.bfloat16), total[1].astype(jnp.bfloat16)
    parts_one, parts_two, returned = lax.optimization_barrier(
        (ring_parts(one, nparts, True), ring_parts(two, nparts, False), returned)
    )
    one, two = ring_sum(one, parts_one), ring_sum(two, parts_two)
    grad_feats = combine_call(send, base.reshape(blocks, BS, dim), returned)
    one = pair_sum(one, nparts, lambda i: i ^ 1, False).astype(jnp.bfloat16)
    two = pair_sum(two, nparts, lambda i: i ^ 1, True).astype(jnp.bfloat16)
    one, two, grad_feats = lax.optimization_barrier((one, two, grad_feats))
    one = pair_sum(one, nparts, lambda i: side - 1 - i, False)
    two = pair_sum(two, nparts, lambda i: side - 1 - i, True)
    half = jnp.stack([one, two])
    other = lax.ppermute(half, "verts", [(v, v ^ 1) for v in range(nparts)])
    first = me % 2 == 0
    q_o = jnp.where(first, half, other)
    k_v = jnp.where(first, other, half)
    grad_weights = jnp.concatenate([q_o[:1], k_v, q_o[1:]], axis=0)
    return (attn_out[None], grad_feats.reshape(1, rows, dim), grad_weights)


def solution(mesh):
    in_specs = (P("dp", "verts", None), P(), P("dp", "verts", None), P(), P())
    out_specs = (P("dp", "verts", None), P("dp", "verts", None), P(None, "dp", None))
    return jax.shard_map(local, mesh=mesh, in_specs=in_specs, out_specs=out_specs, check_vma=False)
```

```python
import functools
import math

import jax
import jax.numpy as jnp
from jax import lax
from jax.experimental import pallas as pl
from jax.experimental.pallas import tpu as pltpu
from jax.sharding import PartitionSpec as P

H = 8
BS = 64
NNB = 8
CAP = 2

ROWS = 1024
PAIR = 4
HALF = 256

NT = (((1,), (1,)), ((), ()))
TN = (((0,), (0,)), ((), ()))


def dot(a, b):
    return jnp.dot(a, b, preferred_element_type=jnp.float32)


def dot_nt(a, b):
    return lax.dot_general(a, b, NT, preferred_element_type=jnp.float32)


def dot_tn(a, b):
    return lax.dot_general(a, b, TN, preferred_element_type=jnp.float32)


def layer_kernel(
    scaling,
    entries,
    counts,
    far_hbm,
    own_k_hbm,
    own_v_hbm,
    wkv_hbm,
    q_hbm,
    u_hbm,
    diag_ref,
    att_hbm,
    gq_hbm,
    gk_hbm,
    gv_hbm,
    own_gk_hbm,
    own_gv_hbm,
    back_hbm,
    far_ref,
    wkv_ref,
    q_ref,
    u_ref,
    att_ref,
    gq_ref,
    keys,
    values,
    gkeys,
    gvalues,
    far_sem,
    in_sem,
    out_sem,
    grad_sem,
):
    parts = far_hbm.shape[0]
    remote = parts * CAP
    table, _, dim = keys.shape
    own = table - remote
    per = ROWS // BS
    half_parts = parts // per
    chunks = remote // per

    def far_copy(i):
        lanes = far_hbm.at[pl.ds(i % half_parts * per, per), i // half_parts]
        return pltpu.make_async_copy(lanes, far_ref.at[pl.ds(i * per, per)], far_sem.at[i])

    def back_copy(i):
        lanes = back_hbm.at[pl.ds(i % half_parts * per, per), i // half_parts]
        return pltpu.make_async_copy(far_ref.at[pl.ds(i * per, per)], lanes, far_sem.at[i])

    def grad_copies(i):
        at = pl.ds(i * per, per)
        return [
            pltpu.make_async_copy(keys.at[at], gk_hbm.at[at], grad_sem.at[0, i]),
            pltpu.make_async_copy(values.at[at], gv_hbm.at[at], grad_sem.at[1, i]),
        ]

    arrive = [
        pltpu.make_async_copy(wkv_hbm, wkv_ref, in_sem.at[0]),
        pltpu.make_async_copy(own_k_hbm, keys.at[pl.ds(remote, own)], in_sem.at[1]),
        pltpu.make_async_copy(own_v_hbm, values.at[pl.ds(remote, own)], in_sem.at[2]),
        pltpu.make_async_copy(q_hbm, q_ref, in_sem.at[3]),
        pltpu.make_async_copy(u_hbm, u_ref, in_sem.at[4]),
    ]
    arrive[0].start()
    for i in range(chunks):
        far_copy(i).start()
    for copy in arrive[1:]:
        copy.start()
    gkeys[pl.ds(remote, own)] = jnp.zeros((own, BS, dim), jnp.float32)
    gvalues[pl.ds(remote, own)] = jnp.zeros((own, BS, dim), jnp.float32)
    arrive[0].wait()

    def project(i, carry):
        first = pl.ds(i * per, per)
        far_copy(i).wait()
        both = dot(far_ref[first].reshape(ROWS, dim), wkv_ref[...]).astype(jnp.bfloat16)
        keys[first] = both[:, :dim].reshape(per, BS, dim)
        values[first] = both[:, dim:].reshape(per, BS, dim)
        gkeys[first] = jnp.zeros((per, BS, dim), jnp.float32)
        gvalues[first] = jnp.zeros((per, BS, dim), jnp.float32)
        return carry

    lax.fori_loop(0, chunks, project, 0)
    for copy in arrive[1:]:
        copy.wait()

    place = lax.broadcasted_iota(jnp.int32, (BS, HALF), 0)
    lane_head = lax.broadcasted_iota(jnp.int32, (BS, HALF), 1) // BS

    def attend(step, carry):
        diag = diag_ref[...]

        def first_half(sub, half):
            at = pl.ds(pl.multiple_of((step * PAIR + sub) * BS, BS), BS)
            cols = slice(half * HALF, (half + 1) * HALF)
            base = (step * PAIR + sub) * NNB
            ids = [entries[base + n] for n in range(NNB)]
            ends = [counts[base + n] for n in range(NNB)]
            queries = q_ref[at, cols] * jnp.bfloat16(scaling)
            qbd = jnp.concatenate([queries] * (HALF // BS), axis=0) * diag
            ubd = jnp.concatenate([u_ref[at, cols]] * (HALF // BS), axis=0) * diag
            k_all = jnp.concatenate([keys[i, :, cols] for i in ids], axis=0)
            v_all = jnp.concatenate([values[i, :, cols] for i in ids], axis=0)
            return at, cols, ids, ends, qbd, ubd, k_all, v_all, dot_nt(k_all, qbd), dot_nt(v_all, ubd)

        def second_half(at, cols, ids, ends, qbd, ubd, k_all, v_all, scores, dprob):
            scores = jnp.concatenate(
                [
                    jnp.where(place < ends[n], scores[n * BS : (n + 1) * BS], -1e30)
                    for n in range(NNB)
                ],
                axis=0,
            )
            top = jnp.max(scores, axis=0, keepdims=True)
            raised = jnp.exp(scores - top)
            probs = raised * (1.0 / jnp.sum(raised, axis=0, keepdims=True))
            probs_b = probs.astype(jnp.bfloat16)
            inner = jnp.sum(probs * dprob, axis=0, keepdims=True)
            dscore = (probs * (dprob - inner)).astype(jnp.bfloat16)
            grad_v = dot(probs_b, ubd)
            grad_k = dot(dscore, qbd)
            att_wide = dot_tn(probs_b, v_all)
            gq_wide = dot_tn(dscore, k_all)
            att = att_wide[:BS]
            gq = gq_wide[:BS]
            for h in range(1, HALF // BS):
                rows = slice(h * BS, (h + 1) * BS)
                att = jnp.where(lane_head == h, att_wide[rows], att)
                gq = jnp.where(lane_head == h, gq_wide[rows], gq)
            att_ref[at, cols] = att.astype(jnp.bfloat16)
            gq_ref[at, cols] = (gq * scaling).astype(jnp.bfloat16)
            for n in range(NNB):
                rows = slice(n * BS, (n + 1) * BS)
                gkeys[ids[n], :, cols] += grad_k[rows]
                gvalues[ids[n], :, cols] += grad_v[rows]

        todo = [(sub, half) for sub in range(PAIR) for half in range(dim // HALF)]
        held = first_half(*todo[0])
        for after in todo[1:] + [None]:
            ahead = first_half(*after) if after else None
            second_half(*held)
            held = ahead
        return carry

    lax.fori_loop(0, own // PAIR, attend, 0)

    leave = [
        pltpu.make_async_copy(att_ref, att_hbm, out_sem.at[0]),
        pltpu.make_async_copy(gq_ref, gq_hbm, out_sem.at[1]),
    ]
    last = pl.ds(remote, own)
    keys[last] = gkeys[last].astype(jnp.bfloat16)
    values[last] = gvalues[last].astype(jnp.bfloat16)
    leave += [
        pltpu.make_async_copy(keys.at[last], own_gk_hbm, out_sem.at[2]),
        pltpu.make_async_copy(values.at[last], own_gv_hbm, out_sem.at[3]),
    ]
    for copy in leave:
        copy.start()

    def send_back(i, carry):
        first = pl.ds(i * per, per)
        grad_k = gkeys[first].astype(jnp.bfloat16)
        grad_v = gvalues[first].astype(jnp.bfloat16)
        keys[first] = grad_k
        values[first] = grad_v
        for copy in grad_copies(i):
            copy.start()
        back = dot_nt(grad_k.reshape(ROWS, dim), wkv_ref[:, :dim]) + dot_nt(
            grad_v.reshape(ROWS, dim), wkv_ref[:, dim:]
        )
        far_ref[first] = back.astype(jnp.bfloat16).reshape(per, BS, dim)
        back_copy(i).start()
        return carry

    lax.fori_loop(0, chunks, send_back, 0)
    for i in range(chunks):
        leave += grad_copies(i) + [back_copy(i)]
    for copy in leave:
        copy.wait()


def layer_call(entries, counts, far, own_k, own_v, wkv, queries, ups, scaling):
    parts, _, _, dim = far.shape
    rows = queries.shape[0]
    own = rows // BS
    table = parts * CAP + own
    chunks = parts * CAP * BS // ROWS
    head = jnp.arange(HALF, dtype=jnp.int32) // BS
    diag = (head[:, None] == head[None, :]).astype(jnp.bfloat16)
    anywhere = pl.BlockSpec(memory_space=pl.ANY)
    return pl.pallas_call(
        functools.partial(layer_kernel, scaling),
        grid_spec=pltpu.PrefetchScalarGridSpec(
            num_scalar_prefetch=2,
            grid=(1,),
            in_specs=[anywhere] * 6 + [pl.BlockSpec((HALF, HALF), lambda i, *_: (0, 0))],
            out_specs=[anywhere] * 7,
            scratch_shapes=[
                pltpu.VMEM((parts * CAP, BS, dim), jnp.bfloat16),
                pltpu.VMEM((dim, 2 * dim), jnp.bfloat16),
                pltpu.VMEM((rows, dim), jnp.bfloat16),
                pltpu.VMEM((rows, dim), jnp.bfloat16),
                pltpu.VMEM((rows, dim), jnp.bfloat16),
                pltpu.VMEM((rows, dim), jnp.bfloat16),
                pltpu.VMEM((table, BS, dim), jnp.bfloat16),
                pltpu.VMEM((table, BS, dim), jnp.bfloat16),
                pltpu.VMEM((table, BS, dim), jnp.float32),
                pltpu.VMEM((table, BS, dim), jnp.float32),
                pltpu.SemaphoreType.DMA((chunks,)),
                pltpu.SemaphoreType.DMA((5,)),
                pltpu.SemaphoreType.DMA((4,)),
                pltpu.SemaphoreType.DMA((2, chunks)),
            ],
        ),
        out_shape=[
            jax.ShapeDtypeStruct((rows, dim), jnp.bfloat16),
            jax.ShapeDtypeStruct((rows, dim), jnp.bfloat16),
            jax.ShapeDtypeStruct((parts * CAP, BS, dim), jnp.bfloat16),
            jax.ShapeDtypeStruct((parts * CAP, BS, dim), jnp.bfloat16),
            jax.ShapeDtypeStruct((own, BS, dim), jnp.bfloat16),
            jax.ShapeDtypeStruct((own, BS, dim), jnp.bfloat16),
            jax.ShapeDtypeStruct(far.shape, jnp.bfloat16),
        ],
        compiler_params=pltpu.CompilerParams(vmem_limit_bytes=60 * 2**20),
    )(entries, counts, far, own_k, own_v, wkv, queries, ups, diag)


def weights_kernel(
    steps_far, core, far_ref, gk_ref, gv_ref, own_gk_ref, own_gv_ref, own_ref, gq_ref, att_ref, cot_ref, mine_ref, give_ref, terms
):
    step = pl.program_id(0)
    rows, dim = own_ref.shape

    @pl.when(step < steps_far)
    def _():
        far = far_ref[...].reshape(ROWS, dim)
        from_k = dot_tn(far, gk_ref[...].reshape(ROWS, dim))
        from_v = dot_tn(far, gv_ref[...].reshape(ROWS, dim))

        @pl.when(step == 0)
        def _():
            terms[2] = from_k
            terms[3] = from_v

        @pl.when(step > 0)
        def _():
            terms[2] += from_k
            terms[3] += from_v

    @pl.when(step == steps_far)
    def _():
        own = own_ref[...]
        terms[0] = dot_tn(own, gq_ref[...])
        terms[1] = dot_tn(att_ref[...], cot_ref[...])
        terms[2] += dot_tn(own, own_gk_ref[...])
        terms[3] += dot_tn(own, own_gv_ref[...])
        mine_ref[...] = terms[pl.ds(2 * core[0], 2)]
        give_ref[...] = terms[pl.ds(2 - 2 * core[0], 2)].astype(jnp.bfloat16)


def weights_call(core, far, grad_k, grad_v, own_gk, own_gv, own, grad_q, attended, cot):
    rows, dim = own.shape
    steps_far = far.shape[0] * CAP * BS // ROWS
    half = steps_far // CAP
    per = ROWS // BS

    def at_far(i, *_):
        chunk = jnp.minimum(i, steps_far - 1)
        return (chunk % half, chunk // half, 0, 0)

    def whole(shape):
        return pl.BlockSpec(shape, lambda i, *_: (0,) * len(shape), pipeline_mode=pl.Buffered(1))

    return pl.pallas_call(
        functools.partial(weights_kernel, steps_far),
        grid_spec=pltpu.PrefetchScalarGridSpec(
            num_scalar_prefetch=1,
            grid=(steps_far + 1,),
            in_specs=[
                pl.BlockSpec((per, None, BS, dim), at_far),
                pl.BlockSpec((per, BS, dim), lambda i, *_: (jnp.minimum(i, steps_far - 1), 0, 0)),
                pl.BlockSpec((per, BS, dim), lambda i, *_: (jnp.minimum(i, steps_far - 1), 0, 0)),
                whole((rows, dim)),
                whole((rows, dim)),
                whole((rows, dim)),
                whole((rows, dim)),
                whole((rows, dim)),
                whole((rows, dim)),
            ],
            out_specs=[whole((2, dim, dim)), whole((2, dim, dim))],
            scratch_shapes=[pltpu.VMEM((4, dim, dim), jnp.float32)],
        ),
        out_shape=[
            jax.ShapeDtypeStruct((2, dim, dim), jnp.float32),
            jax.ShapeDtypeStruct((2, dim, dim), jnp.bfloat16),
        ],
        compiler_params=pltpu.CompilerParams(vmem_limit_bytes=60 * 2**20),
        cost_estimate=pl.CostEstimate(flops=11 * 10**9, bytes_accessed=20 * 10**6, transcendentals=0),
    )(core, far, grad_k, grad_v, own_gk, own_gv, own, grad_q, attended, cot)


def combine_kernel(per, send_ref, base_ref, returned_ref, out_ref, acc):
    step = pl.program_id(0)

    @pl.when(step == 0)
    def _():
        acc[...] = base_ref[...]

    for i in range(per):
        for c in range(CAP):
            acc[send_ref[c, step * per + i]] += returned_ref[i, c].astype(jnp.float32)

    @pl.when(step == pl.num_programs(0) - 1)
    def _():
        out_ref[...] = acc[...].astype(jnp.bfloat16)


def combine_call(send, base, returned):
    blocks, _, dim = base.shape
    parts = returned.shape[0]
    per = 8
    return pl.pallas_call(
        functools.partial(combine_kernel, per),
        grid_spec=pltpu.PrefetchScalarGridSpec(
            num_scalar_prefetch=1,
            grid=(parts // per,),
            in_specs=[
                pl.BlockSpec((blocks, BS, dim), lambda i, *_: (0, 0, 0)),
                pl.BlockSpec((per, CAP, BS, dim), lambda i, *_: (i, 0, 0, 0)),
            ],
            out_specs=pl.BlockSpec((blocks, BS, dim), lambda i, *_: (0, 0, 0)),
            scratch_shapes=[pltpu.VMEM((blocks, BS, dim), jnp.float32)],
        ),
        out_shape=jax.ShapeDtypeStruct((blocks, BS, dim), jnp.bfloat16),
        compiler_params=pltpu.CompilerParams(vmem_limit_bytes=32 * 2**20),
    )(send, base, returned)


def over_cores_and_planes(mine, give, nparts):
    half = mine + lax.ppermute(give, "verts", [(v, v ^ 1) for v in range(nparts)]).astype(jnp.float32)
    planes = lax.axis_size("dp")
    here = lax.axis_index("dp")
    rows = half.shape[1] // planes
    total = lax.dynamic_slice_in_dim(half, here * rows, rows, 1)
    for d in range(1, planes):
        there = lax.dynamic_slice_in_dim(half, (here + d) % planes * rows, rows, 1)
        move = [(z, (z + d) % planes) for z in range(planes)]
        total += lax.ppermute(there.astype(jnp.bfloat16), "dp", move).astype(jnp.float32)
    return total


def moved(nparts, dx, dy):
    side = math.isqrt(nparts // 2)
    wide = nparts // side

    def go(i, d):
        return d(i) if callable(d) else (i + d) % side

    return [
        (v, go(v // wide, dy) * wide + go(v % wide // 2, dx) * 2 + v % 2) for v in range(nparts)
    ]


def ring_parts(value, nparts, along_x):
    side = math.isqrt(nparts // 2)
    moves = [moved(nparts, d, 0) if along_x else moved(nparts, 0, d) for d in range(1, side)]
    return [lax.ppermute(value, "verts", move) for move in moves]


def ring_sum(value, parts):
    one, two, three = [part.astype(jnp.float32) for part in parts]
    return ((value.astype(jnp.float32) + two) + (one + three)).astype(jnp.bfloat16)


def pair_sum(value, nparts, partner, along_x):
    move = moved(nparts, partner, 0) if along_x else moved(nparts, 0, partner)
    return value.astype(jnp.float32) + lax.ppermute(value, "verts", move).astype(jnp.float32)


def local(feats, weights, grad_out, neighbours, valid):
    nparts = lax.axis_size("verts")
    me = lax.axis_index("verts")
    _, rows, dim = feats.shape
    blocks = rows // BS
    scaling = 1.0 / math.sqrt(dim // H)
    part_ids = jnp.arange(nparts, dtype=jnp.int32)
    inputs_now = feats[0]
    cotangent = grad_out[0]
    w_kv = jnp.concatenate([weights[1], weights[2]], axis=1)

    theirs = neighbours.reshape(nparts, blocks * NNB)
    mine = (theirs // blocks == me) & (part_ids[:, None] != me)
    place = theirs % blocks
    low = jnp.min(jnp.where(mine, place, blocks), axis=1)
    high = jnp.max(jnp.where(mine, place, -1), axis=1)
    send = jnp.stack([low % blocks, jnp.maximum(high, 0)])

    lists = lax.dynamic_slice_in_dim(neighbours, me * blocks, blocks, 0).reshape(-1)
    owner = lists // blocks
    named = owner[:, None] == part_ids[None, :]
    lower = jnp.min(jnp.where(named, (lists % blocks)[:, None], blocks), axis=0)
    slot = (jnp.sum(jnp.where(named, lower[None, :], 0), axis=1) != lists % blocks).astype(jnp.int32)
    entries = jnp.where(owner == me, nparts * CAP + lists % blocks, slot * nparts + owner)
    counts = jnp.sum(valid, axis=1)[lists]

    far = lax.all_to_all(
        inputs_now.reshape(blocks, BS, dim)[send.T.reshape(-1)].reshape(nparts, CAP, BS, dim),
        "verts",
        split_axis=0,
        concat_axis=0,
        tiled=True,
    )

    queries = dot(inputs_now, weights[0]).astype(jnp.bfloat16)
    ups = dot_nt(cotangent, weights[3]).astype(jnp.bfloat16)
    own_k = dot(inputs_now, weights[1]).astype(jnp.bfloat16).reshape(blocks, BS, dim)
    own_v = dot(inputs_now, weights[2]).astype(jnp.bfloat16).reshape(blocks, BS, dim)

    attended, grad_q, grad_k, grad_v, own_gk, own_gv, back = layer_call(
        entries, counts, far, own_k, own_v, w_kv, queries, ups, scaling
    )
    own_gk, own_gv = own_gk.reshape(rows, dim), own_gv.reshape(rows, dim)
    returned = lax.all_to_all(back, "verts", split_axis=0, concat_axis=0, tiled=True)
    mine, give = weights_call(
        (me % 2).reshape(1),
        far,
        grad_k,
        grad_v,
        own_gk,
        own_gv,
        inputs_now,
        grad_q,
        attended,
        cotangent,
    )
    total = over_cores_and_planes(mine, give, nparts)
    attn_out = dot(attended, weights[3]).astype(jnp.bfloat16)
    base = dot_nt(grad_q, weights[0]) + dot_nt(own_gk, weights[1]) + dot_nt(own_gv, weights[2])
    total, attn_out, base = lax.optimization_barrier((total, attn_out, base))

    side = math.isqrt(nparts // 2)
    one, two = total[0].astype(jnp.bfloat16), total[1].astype(jnp.bfloat16)
    parts_one, parts_two, returned = lax.optimization_barrier(
        (ring_parts(one, nparts, True), ring_parts(two, nparts, False), returned)
    )
    one, two = ring_sum(one, parts_one), ring_sum(two, parts_two)
    grad_feats = combine_call(send, base.reshape(blocks, BS, dim), returned)
    one = pair_sum(one, nparts, lambda i: i ^ 1, False).astype(jnp.bfloat16)
    two = pair_sum(two, nparts, lambda i: i ^ 1, True).astype(jnp.bfloat16)
    one, two, grad_feats = lax.optimization_barrier((one, two, grad_feats))
    one = pair_sum(one, nparts, lambda i: side - 1 - i, False)
    two = pair_sum(two, nparts, lambda i: side - 1 - i, True)
    half = jnp.stack([one, two])
    other = lax.ppermute(half, "verts", [(v, v ^ 1) for v in range(nparts)])
    first = me % 2 == 0
    q_o = jnp.where(first, half, other)
    k_v = jnp.where(first, other, half)
    grad_weights = jnp.concatenate([q_o[:1], k_v, q_o[1:]], axis=0)
    return (attn_out[None], grad_feats.reshape(1, rows, dim), grad_weights)


def solution(mesh):
    in_specs = (P("dp", "verts", None), P(), P("dp", "verts", None), P(), P())
    out_specs = (P("dp", "verts", None), P("dp", "verts", None), P(None, "dp", None))
    return jax.shard_map(local, mesh=mesh, in_specs=in_specs, out_specs=out_specs, check_vma=False)
```

```python
import functools
import math

import jax
import jax.numpy as jnp
from jax import lax
from jax.experimental import pallas as pl
from jax.experimental.pallas import tpu as pltpu
from jax.sharding import PartitionSpec as P

H = 8
BS = 64
NNB = 8
CAP = 2

ROWS = 1024
PAIR = 4
HALF = 256

NT = (((1,), (1,)), ((), ()))
TN = (((0,), (0,)), ((), ()))


def dot(a, b):
    return jnp.dot(a, b, preferred_element_type=jnp.float32)


def dot_nt(a, b):
    return lax.dot_general(a, b, NT, preferred_element_type=jnp.float32)


def dot_tn(a, b):
    return lax.dot_general(a, b, TN, preferred_element_type=jnp.float32)


def layer_kernel(
    scaling,
    entries,
    counts,
    far_hbm,
    own_k_hbm,
    own_v_hbm,
    wkv_hbm,
    q_hbm,
    u_hbm,
    diag_ref,
    att_hbm,
    gq_hbm,
    gk_hbm,
    gv_hbm,
    own_gk_hbm,
    own_gv_hbm,
    back_hbm,
    far_ref,
    wkv_ref,
    q_ref,
    u_ref,
    att_ref,
    gq_ref,
    keys,
    values,
    gkeys,
    gvalues,
    far_sem,
    in_sem,
    out_sem,
    grad_sem,
):
    parts = far_hbm.shape[0]
    remote = parts * CAP
    table, _, dim = keys.shape
    own = table - remote
    per = ROWS // BS
    half_parts = parts // per
    chunks = remote // per

    def far_copy(i):
        lanes = far_hbm.at[pl.ds(i % half_parts * per, per), i // half_parts]
        return pltpu.make_async_copy(lanes, far_ref.at[pl.ds(i * per, per)], far_sem.at[i])

    def back_copy(i):
        lanes = back_hbm.at[pl.ds(i % half_parts * per, per), i // half_parts]
        return pltpu.make_async_copy(far_ref.at[pl.ds(i * per, per)], lanes, far_sem.at[i])

    def grad_copies(i):
        at = pl.ds(i * per, per)
        return [
            pltpu.make_async_copy(keys.at[at], gk_hbm.at[at], grad_sem.at[0, i]),
            pltpu.make_async_copy(values.at[at], gv_hbm.at[at], grad_sem.at[1, i]),
        ]

    arrive = [
        pltpu.make_async_copy(wkv_hbm, wkv_ref, in_sem.at[0]),
        pltpu.make_async_copy(own_k_hbm, keys.at[pl.ds(remote, own)], in_sem.at[1]),
        pltpu.make_async_copy(own_v_hbm, values.at[pl.ds(remote, own)], in_sem.at[2]),
        pltpu.make_async_copy(q_hbm, q_ref, in_sem.at[3]),
        pltpu.make_async_copy(u_hbm, u_ref, in_sem.at[4]),
    ]
    arrive[0].start()
    for i in range(chunks):
        far_copy(i).start()
    for copy in arrive[1:]:
        copy.start()
    gkeys[pl.ds(remote, own)] = jnp.zeros((own, BS, dim), jnp.float32)
    gvalues[pl.ds(remote, own)] = jnp.zeros((own, BS, dim), jnp.float32)
    arrive[0].wait()

    def project(i, carry):
        first = pl.ds(i * per, per)
        far_copy(i).wait()
        both = dot(far_ref[first].reshape(ROWS, dim), wkv_ref[...]).astype(jnp.bfloat16)
        keys[first] = both[:, :dim].reshape(per, BS, dim)
        values[first] = both[:, dim:].reshape(per, BS, dim)
        gkeys[first] = jnp.zeros((per, BS, dim), jnp.float32)
        gvalues[first] = jnp.zeros((per, BS, dim), jnp.float32)
        return carry

    lax.fori_loop(0, chunks, project, 0)
    for copy in arrive[1:]:
        copy.wait()

    place = lax.broadcasted_iota(jnp.int32, (BS, HALF), 0)
    lane_head = lax.broadcasted_iota(jnp.int32, (BS, HALF), 1) // BS

    def attend(step, carry):
        diag = diag_ref[...]

        def first_half(sub, half):
            at = pl.ds(pl.multiple_of((step * PAIR + sub) * BS, BS), BS)
            cols = slice(half * HALF, (half + 1) * HALF)
            base = (step * PAIR + sub) * NNB
            ids = [entries[base + n] for n in range(NNB)]
            ends = [counts[base + n] for n in range(NNB)]
            queries = q_ref[at, cols] * jnp.bfloat16(scaling)
            qbd = jnp.concatenate([queries] * (HALF // BS), axis=0) * diag
            ubd = jnp.concatenate([u_ref[at, cols]] * (HALF // BS), axis=0) * diag
            k_all = jnp.concatenate([keys[i, :, cols] for i in ids], axis=0)
            v_all = jnp.concatenate([values[i, :, cols] for i in ids], axis=0)
            return at, cols, ids, ends, qbd, ubd, k_all, v_all, dot_nt(k_all, qbd), dot_nt(v_all, ubd)

        def second_half(at, cols, ids, ends, qbd, ubd, k_all, v_all, scores, dprob):
            scores = jnp.concatenate(
                [
                    jnp.where(place < ends[n], scores[n * BS : (n + 1) * BS], -1e30)
                    for n in range(NNB)
                ],
                axis=0,
            )
            top = jnp.max(scores, axis=0, keepdims=True)
            raised = jnp.exp(scores - top)
            probs = raised * (1.0 / jnp.sum(raised, axis=0, keepdims=True))
            probs_b = probs.astype(jnp.bfloat16)
            inner = jnp.sum(probs * dprob, axis=0, keepdims=True)
            dscore = (probs * (dprob - inner)).astype(jnp.bfloat16)
            grad_v = dot(probs_b, ubd)
            grad_k = dot(dscore, qbd)
            att_wide = dot_tn(probs_b, v_all)
            gq_wide = dot_tn(dscore, k_all)
            att = att_wide[:BS]
            gq = gq_wide[:BS]
            for h in range(1, HALF // BS):
                rows = slice(h * BS, (h + 1) * BS)
                att = jnp.where(lane_head == h, att_wide[rows], att)
                gq = jnp.where(lane_head == h, gq_wide[rows], gq)
            att_ref[at, cols] = att.astype(jnp.bfloat16)
            gq_ref[at, cols] = (gq * scaling).astype(jnp.bfloat16)
            for n in range(NNB):
                rows = slice(n * BS, (n + 1) * BS)
                gkeys[ids[n], :, cols] += grad_k[rows]
                gvalues[ids[n], :, cols] += grad_v[rows]

        todo = [(sub, half) for sub in range(PAIR) for half in range(dim // HALF)]
        held = first_half(*todo[0])
        for after in todo[1:] + [None]:
            ahead = first_half(*after) if after else None
            second_half(*held)
            held = ahead
        return carry

    lax.fori_loop(0, own // PAIR, attend, 0)

    leave = [
        pltpu.make_async_copy(att_ref, att_hbm, out_sem.at[0]),
        pltpu.make_async_copy(gq_ref, gq_hbm, out_sem.at[1]),
    ]
    last = pl.ds(remote, own)
    keys[last] = gkeys[last].astype(jnp.bfloat16)
    values[last] = gvalues[last].astype(jnp.bfloat16)
    leave += [
        pltpu.make_async_copy(keys.at[last], own_gk_hbm, out_sem.at[2]),
        pltpu.make_async_copy(values.at[last], own_gv_hbm, out_sem.at[3]),
    ]
    for copy in leave:
        copy.start()

    def send_back(i, carry):
        first = pl.ds(i * per, per)
        grad_k = gkeys[first].astype(jnp.bfloat16)
        grad_v = gvalues[first].astype(jnp.bfloat16)
        keys[first] = grad_k
        values[first] = grad_v
        for copy in grad_copies(i):
            copy.start()
        back = dot_nt(grad_k.reshape(ROWS, dim), wkv_ref[:, :dim]) + dot_nt(
            grad_v.reshape(ROWS, dim), wkv_ref[:, dim:]
        )
        far_ref[first] = back.astype(jnp.bfloat16).reshape(per, BS, dim)
        back_copy(i).start()
        return carry

    lax.fori_loop(0, chunks, send_back, 0)
    for i in range(chunks):
        leave += grad_copies(i) + [back_copy(i)]
    for copy in leave:
        copy.wait()


def layer_call(entries, counts, far, own_k, own_v, wkv, queries, ups, scaling):
    parts, _, _, dim = far.shape
    rows = queries.shape[0]
    own = rows // BS
    table = parts * CAP + own
    chunks = parts * CAP * BS // ROWS
    head = jnp.arange(HALF, dtype=jnp.int32) // BS
    diag = (head[:, None] == head[None, :]).astype(jnp.bfloat16)
    anywhere = pl.BlockSpec(memory_space=pl.ANY)
    return pl.pallas_call(
        functools.partial(layer_kernel, scaling),
        grid_spec=pltpu.PrefetchScalarGridSpec(
            num_scalar_prefetch=2,
            grid=(1,),
            in_specs=[anywhere] * 6 + [pl.BlockSpec((HALF, HALF), lambda i, *_: (0, 0))],
            out_specs=[anywhere] * 7,
            scratch_shapes=[
                pltpu.VMEM((parts * CAP, BS, dim), jnp.bfloat16),
                pltpu.VMEM((dim, 2 * dim), jnp.bfloat16),
                pltpu.VMEM((rows, dim), jnp.bfloat16),
                pltpu.VMEM((rows, dim), jnp.bfloat16),
                pltpu.VMEM((rows, dim), jnp.bfloat16),
                pltpu.VMEM((rows, dim), jnp.bfloat16),
                pltpu.VMEM((table, BS, dim), jnp.bfloat16),
                pltpu.VMEM((table, BS, dim), jnp.bfloat16),
                pltpu.VMEM((table, BS, dim), jnp.float32),
                pltpu.VMEM((table, BS, dim), jnp.float32),
                pltpu.SemaphoreType.DMA((chunks,)),
                pltpu.SemaphoreType.DMA((5,)),
                pltpu.SemaphoreType.DMA((4,)),
                pltpu.SemaphoreType.DMA((2, chunks)),
            ],
        ),
        out_shape=[
            jax.ShapeDtypeStruct((rows, dim), jnp.bfloat16),
            jax.ShapeDtypeStruct((rows, dim), jnp.bfloat16),
            jax.ShapeDtypeStruct((parts * CAP, BS, dim), jnp.bfloat16),
            jax.ShapeDtypeStruct((parts * CAP, BS, dim), jnp.bfloat16),
            jax.ShapeDtypeStruct((own, BS, dim), jnp.bfloat16),
            jax.ShapeDtypeStruct((own, BS, dim), jnp.bfloat16),
            jax.ShapeDtypeStruct(far.shape, jnp.bfloat16),
        ],
        compiler_params=pltpu.CompilerParams(vmem_limit_bytes=60 * 2**20),
    )(entries, counts, far, own_k, own_v, wkv, queries, ups, diag)


def weights_kernel(
    steps_far, core, far_ref, gk_ref, gv_ref, own_gk_ref, own_gv_ref, own_ref, gq_ref, att_ref, cot_ref, mine_ref, give_ref, terms
):
    step = pl.program_id(0)
    rows, dim = own_ref.shape

    @pl.when(step < steps_far)
    def _():
        far = far_ref[...].reshape(ROWS, dim)
        from_k = dot_tn(far, gk_ref[...].reshape(ROWS, dim))
        from_v = dot_tn(far, gv_ref[...].reshape(ROWS, dim))

        @pl.when(step == 0)
        def _():
            terms[2] = from_k
            terms[3] = from_v

        @pl.when(step > 0)
        def _():
            terms[2] += from_k
            terms[3] += from_v

    @pl.when(step == steps_far)
    def _():
        own = own_ref[...]
        terms[0] = dot_tn(own, gq_ref[...])
        terms[1] = dot_tn(att_ref[...], cot_ref[...])
        terms[2] += dot_tn(own, own_gk_ref[...])
        terms[3] += dot_tn(own, own_gv_ref[...])
        mine_ref[...] = terms[pl.ds(2 * core[0], 2)]
        give_ref[...] = terms[pl.ds(2 - 2 * core[0], 2)].astype(jnp.bfloat16)


def weights_call(core, far, grad_k, grad_v, own_gk, own_gv, own, grad_q, attended, cot):
    rows, dim = own.shape
    steps_far = far.shape[0] * CAP * BS // ROWS
    half = steps_far // CAP
    per = ROWS // BS

    def at_far(i, *_):
        chunk = jnp.minimum(i, steps_far - 1)
        return (chunk % half, chunk // half, 0, 0)

    def whole(shape):
        return pl.BlockSpec(shape, lambda i, *_: (0,) * len(shape), pipeline_mode=pl.Buffered(1))

    return pl.pallas_call(
        functools.partial(weights_kernel, steps_far),
        grid_spec=pltpu.PrefetchScalarGridSpec(
            num_scalar_prefetch=1,
            grid=(steps_far + 1,),
            in_specs=[
                pl.BlockSpec((per, None, BS, dim), at_far),
                pl.BlockSpec((per, BS, dim), lambda i, *_: (jnp.minimum(i, steps_far - 1), 0, 0)),
                pl.BlockSpec((per, BS, dim), lambda i, *_: (jnp.minimum(i, steps_far - 1), 0, 0)),
                whole((rows, dim)),
                whole((rows, dim)),
                whole((rows, dim)),
                whole((rows, dim)),
                whole((rows, dim)),
                whole((rows, dim)),
            ],
            out_specs=[whole((2, dim, dim)), whole((2, dim, dim))],
            scratch_shapes=[pltpu.VMEM((4, dim, dim), jnp.float32)],
        ),
        out_shape=[
            jax.ShapeDtypeStruct((2, dim, dim), jnp.float32),
            jax.ShapeDtypeStruct((2, dim, dim), jnp.bfloat16),
        ],
        compiler_params=pltpu.CompilerParams(vmem_limit_bytes=60 * 2**20),
        cost_estimate=pl.CostEstimate(flops=11 * 10**9, bytes_accessed=20 * 10**6, transcendentals=0),
    )(core, far, grad_k, grad_v, own_gk, own_gv, own, grad_q, attended, cot)


def combine_kernel(per, send_ref, base_ref, returned_ref, out_ref, acc):
    step = pl.program_id(0)

    @pl.when(step == 0)
    def _():
        acc[...] = base_ref[...]

    for i in range(per):
        for c in range(CAP):
            acc[send_ref[c, step * per + i]] += returned_ref[i, c].astype(jnp.float32)

    @pl.when(step == pl.num_programs(0) - 1)
    def _():
        out_ref[...] = acc[...].astype(jnp.bfloat16)


def combine_call(send, base, returned):
    blocks, _, dim = base.shape
    parts = returned.shape[0]
    per = 8
    return pl.pallas_call(
        functools.partial(combine_kernel, per),
        grid_spec=pltpu.PrefetchScalarGridSpec(
            num_scalar_prefetch=1,
            grid=(parts // per,),
            in_specs=[
                pl.BlockSpec((blocks, BS, dim), lambda i, *_: (0, 0, 0)),
                pl.BlockSpec((per, CAP, BS, dim), lambda i, *_: (i, 0, 0, 0)),
            ],
            out_specs=pl.BlockSpec((blocks, BS, dim), lambda i, *_: (0, 0, 0)),
            scratch_shapes=[pltpu.VMEM((blocks, BS, dim), jnp.float32)],
        ),
        out_shape=jax.ShapeDtypeStruct((blocks, BS, dim), jnp.bfloat16),
        compiler_params=pltpu.CompilerParams(vmem_limit_bytes=32 * 2**20),
    )(send, base, returned)


def over_cores_and_planes(mine, give, nparts):
    half = mine + lax.ppermute(give, "verts", [(v, v ^ 1) for v in range(nparts)]).astype(jnp.float32)
    planes = lax.axis_size("dp")
    here = lax.axis_index("dp")
    rows = half.shape[1] // planes
    total = lax.dynamic_slice_in_dim(half, here * rows, rows, 1)
    for d in range(1, planes):
        there = lax.dynamic_slice_in_dim(half, (here + d) % planes * rows, rows, 1)
        move = [(z, (z + d) % planes) for z in range(planes)]
        total += lax.ppermute(there.astype(jnp.bfloat16), "dp", move).astype(jnp.float32)
    return total


def moved(nparts, dx, dy):
    side = math.isqrt(nparts // 2)
    wide = nparts // side

    def go(i, d):
        return d(i) if callable(d) else (i + d) % side

    return [
        (v, go(v // wide, dy) * wide + go(v % wide // 2, dx) * 2 + v % 2) for v in range(nparts)
    ]


def ring_parts(value, nparts, along_x):
    side = math.isqrt(nparts // 2)
    moves = [moved(nparts, d, 0) if along_x else moved(nparts, 0, d) for d in range(1, side)]
    return [lax.ppermute(value, "verts", move) for move in moves]


def ring_sum(value, parts):
    one, two, three = [part.astype(jnp.float32) for part in parts]
    return ((value.astype(jnp.float32) + two) + (one + three)).astype(jnp.bfloat16)


def pair_sum(value, nparts, partner, along_x):
    move = moved(nparts, partner, 0) if along_x else moved(nparts, 0, partner)
    return value.astype(jnp.float32) + lax.ppermute(value, "verts", move).astype(jnp.float32)


def local(feats, weights, grad_out, neighbours, valid):
    nparts = lax.axis_size("verts")
    me = lax.axis_index("verts")
    _, rows, dim = feats.shape
    blocks = rows // BS
    scaling = 1.0 / math.sqrt(dim // H)
    part_ids = jnp.arange(nparts, dtype=jnp.int32)
    inputs_now = feats[0]
    cotangent = grad_out[0]
    w_kv = jnp.concatenate([weights[1], weights[2]], axis=1)

    theirs = neighbours.reshape(nparts, blocks * NNB)
    mine = (theirs // blocks == me) & (part_ids[:, None] != me)
    place = theirs % blocks
    low = jnp.min(jnp.where(mine, place, blocks), axis=1)
    high = jnp.max(jnp.where(mine, place, -1), axis=1)
    send = jnp.stack([low % blocks, jnp.maximum(high, 0)])

    lists = lax.dynamic_slice_in_dim(neighbours, me * blocks, blocks, 0).reshape(-1)
    owner = lists // blocks
    named = owner[:, None] == part_ids[None, :]
    lower = jnp.min(jnp.where(named, (lists % blocks)[:, None], blocks), axis=0)
    slot = (jnp.sum(jnp.where(named, lower[None, :], 0), axis=1) != lists % blocks).astype(jnp.int32)
    entries = jnp.where(owner == me, nparts * CAP + lists % blocks, slot * nparts + owner)
    counts = jnp.sum(valid, axis=1)[lists]

    far = lax.all_to_all(
        inputs_now.reshape(blocks, BS, dim)[send.T.reshape(-1)].reshape(nparts, CAP, BS, dim),
        "verts",
        split_axis=0,
        concat_axis=0,
        tiled=True,
    )

    queries = dot(inputs_now, weights[0]).astype(jnp.bfloat16)
    ups = dot_nt(cotangent, weights[3]).astype(jnp.bfloat16)
    own_k = dot(inputs_now, weights[1]).astype(jnp.bfloat16).reshape(blocks, BS, dim)
    own_v = dot(inputs_now, weights[2]).astype(jnp.bfloat16).reshape(blocks, BS, dim)

    attended, grad_q, grad_k, grad_v, own_gk, own_gv, back = layer_call(
        entries, counts, far, own_k, own_v, w_kv, queries, ups, scaling
    )
    own_gk, own_gv = own_gk.reshape(rows, dim), own_gv.reshape(rows, dim)
    returned = lax.all_to_all(back, "verts", split_axis=0, concat_axis=0, tiled=True)
    mine, give = weights_call(
        (me % 2).reshape(1),
        far,
        grad_k,
        grad_v,
        own_gk,
        own_gv,
        inputs_now,
        grad_q,
        attended,
        cotangent,
    )
    total = over_cores_and_planes(mine, give, nparts)
    attn_out = dot(attended, weights[3]).astype(jnp.bfloat16)
    base = dot_nt(grad_q, weights[0]) + dot_nt(own_gk, weights[1]) + dot_nt(own_gv, weights[2])
    total, attn_out, base = lax.optimization_barrier((total, attn_out, base))

    side = math.isqrt(nparts // 2)
    one, two = total[0].astype(jnp.bfloat16), total[1].astype(jnp.bfloat16)
    parts_one, parts_two, returned = lax.optimization_barrier(
        (ring_parts(one, nparts, True), ring_parts(two, nparts, False), returned)
    )
    one, two = ring_sum(one, parts_one), ring_sum(two, parts_two)
    grad_feats = combine_call(send, base.reshape(blocks, BS, dim), returned)
    one = pair_sum(one, nparts, lambda i: i ^ 1, False).astype(jnp.bfloat16)
    two = pair_sum(two, nparts, lambda i: i ^ 1, True).astype(jnp.bfloat16)
    one, two, grad_feats = lax.optimization_barrier((one, two, grad_feats))
    one = pair_sum(one, nparts, lambda i: side - 1 - i, False)
    two = pair_sum(two, nparts, lambda i: side - 1 - i, True)
    half = jnp.stack([one, two]).astype(jnp.bfloat16)
    other = lax.ppermute(half, "verts", [(v, v ^ 1) for v in range(nparts)])
    first = me % 2 == 0
    q_o = jnp.where(first, half, other).astype(jnp.float32)
    k_v = jnp.where(first, other, half).astype(jnp.float32)
    grad_weights = jnp.concatenate([q_o[:1], k_v, q_o[1:]], axis=0)
    return (attn_out[None], grad_feats.reshape(1, rows, dim), grad_weights)


def solution(mesh):
    in_specs = (P("dp", "verts", None), P(), P("dp", "verts", None), P(), P())
    out_specs = (P("dp", "verts", None), P("dp", "verts", None), P(None, "dp", None))
    return jax.shard_map(local, mesh=mesh, in_specs=in_specs, out_specs=out_specs, check_vma=False)
```

```python
import functools
import math

import jax
import jax.numpy as jnp
from jax import lax
from jax.experimental import pallas as pl
from jax.experimental.pallas import tpu as pltpu
from jax.sharding import PartitionSpec as P

H = 8
BS = 64
NNB = 8
CAP = 2

ROWS = 1024
PAIR = 4
HALF = 256

NT = (((1,), (1,)), ((), ()))
TN = (((0,), (0,)), ((), ()))


def dot(a, b):
    return jnp.dot(a, b, preferred_element_type=jnp.float32)


def dot_nt(a, b):
    return lax.dot_general(a, b, NT, preferred_element_type=jnp.float32)


def dot_tn(a, b):
    return lax.dot_general(a, b, TN, preferred_element_type=jnp.float32)


def layer_kernel(
    scaling,
    entries,
    counts,
    far_hbm,
    own_k_hbm,
    own_v_hbm,
    wkv_hbm,
    q_hbm,
    u_hbm,
    diag_ref,
    att_hbm,
    gq_hbm,
    gk_hbm,
    gv_hbm,
    own_gk_hbm,
    own_gv_hbm,
    back_hbm,
    far_ref,
    wkv_ref,
    q_ref,
    u_ref,
    att_ref,
    gq_ref,
    keys,
    values,
    gkeys,
    gvalues,
    far_sem,
    in_sem,
    out_sem,
    grad_sem,
):
    parts = far_hbm.shape[0]
    remote = parts * CAP
    table, _, dim = keys.shape
    own = table - remote
    per = ROWS // BS
    half_parts = parts // per
    chunks = remote // per

    def far_copy(i):
        lanes = far_hbm.at[pl.ds(i % half_parts * per, per), i // half_parts]
        return pltpu.make_async_copy(lanes, far_ref.at[pl.ds(i * per, per)], far_sem.at[i])

    def back_copy(i):
        lanes = back_hbm.at[pl.ds(i % half_parts * per, per), i // half_parts]
        return pltpu.make_async_copy(far_ref.at[pl.ds(i * per, per)], lanes, far_sem.at[i])

    def grad_copies(i):
        at = pl.ds(i * per, per)
        return [
            pltpu.make_async_copy(keys.at[at], gk_hbm.at[at], grad_sem.at[0, i]),
            pltpu.make_async_copy(values.at[at], gv_hbm.at[at], grad_sem.at[1, i]),
        ]

    arrive = [
        pltpu.make_async_copy(wkv_hbm, wkv_ref, in_sem.at[0]),
        pltpu.make_async_copy(own_k_hbm, keys.at[pl.ds(remote, own)], in_sem.at[1]),
        pltpu.make_async_copy(own_v_hbm, values.at[pl.ds(remote, own)], in_sem.at[2]),
        pltpu.make_async_copy(q_hbm, q_ref, in_sem.at[3]),
        pltpu.make_async_copy(u_hbm, u_ref, in_sem.at[4]),
    ]
    arrive[0].start()
    for i in range(chunks):
        far_copy(i).start()
    for copy in arrive[1:]:
        copy.start()
    gkeys[pl.ds(remote, own)] = jnp.zeros((own, BS, dim), jnp.float32)
    gvalues[pl.ds(remote, own)] = jnp.zeros((own, BS, dim), jnp.float32)
    arrive[0].wait()

    def project(i, carry):
        first = pl.ds(i * per, per)
        far_copy(i).wait()
        both = dot(far_ref[first].reshape(ROWS, dim), wkv_ref[...]).astype(jnp.bfloat16)
        keys[first] = both[:, :dim].reshape(per, BS, dim)
        values[first] = both[:, dim:].reshape(per, BS, dim)
        gkeys[first] = jnp.zeros((per, BS, dim), jnp.float32)
        gvalues[first] = jnp.zeros((per, BS, dim), jnp.float32)
        return carry

    lax.fori_loop(0, chunks, project, 0)
    for copy in arrive[1:]:
        copy.wait()

    place = lax.broadcasted_iota(jnp.int32, (BS, HALF), 0)
    lane_head = lax.broadcasted_iota(jnp.int32, (BS, HALF), 1) // BS

    def attend(step, carry):
        diag = diag_ref[...]

        def first_half(sub, half):
            at = pl.ds(pl.multiple_of((step * PAIR + sub) * BS, BS), BS)
            cols = slice(half * HALF, (half + 1) * HALF)
            base = (step * PAIR + sub) * NNB
            ids = [entries[base + n] for n in range(NNB)]
            ends = [counts[base + n] for n in range(NNB)]
            queries = q_ref[at, cols] * jnp.bfloat16(scaling)
            qbd = jnp.concatenate([queries] * (HALF // BS), axis=0) * diag
            ubd = jnp.concatenate([u_ref[at, cols]] * (HALF // BS), axis=0) * diag
            k_all = jnp.concatenate([keys[i, :, cols] for i in ids], axis=0)
            v_all = jnp.concatenate([values[i, :, cols] for i in ids], axis=0)
            return at, cols, ids, ends, qbd, ubd, k_all, v_all, dot_nt(k_all, qbd), dot_nt(v_all, ubd)

        def second_half(at, cols, ids, ends, qbd, ubd, k_all, v_all, scores, dprob):
            scores = jnp.concatenate(
                [
                    piece
                    for n in range(NNB)
                    for piece in (
                        scores[n * BS : n * BS + BS // 2],
                        jnp.where(
                            place[BS // 2 :] < ends[n],
                            scores[n * BS + BS // 2 : (n + 1) * BS],
                            -1e30,
                        ),
                    )
                ],
                axis=0,
            )
            top = jnp.max(scores, axis=0, keepdims=True)
            raised = jnp.exp(scores - top)
            probs = raised * (1.0 / jnp.sum(raised, axis=0, keepdims=True))
            probs_b = probs.astype(jnp.bfloat16)
            inner = jnp.sum(probs * dprob, axis=0, keepdims=True)
            dscore = (probs * (dprob - inner)).astype(jnp.bfloat16)
            grad_v = dot(probs_b, ubd)
            grad_k = dot(dscore, qbd)
            att_wide = dot_tn(probs_b, v_all)
            gq_wide = dot_tn(dscore, k_all)
            att = att_wide[:BS]
            gq = gq_wide[:BS]
            for h in range(1, HALF // BS):
                rows = slice(h * BS, (h + 1) * BS)
                att = jnp.where(lane_head == h, att_wide[rows], att)
                gq = jnp.where(lane_head == h, gq_wide[rows], gq)
            att_ref[at, cols] = att.astype(jnp.bfloat16)
            gq_ref[at, cols] = (gq * scaling).astype(jnp.bfloat16)
            for n in range(NNB):
                rows = slice(n * BS, (n + 1) * BS)
                gkeys[ids[n], :, cols] += grad_k[rows]
                gvalues[ids[n], :, cols] += grad_v[rows]

        todo = [(sub, half) for sub in range(PAIR) for half in range(dim // HALF)]
        held = first_half(*todo[0])
        for after in todo[1:] + [None]:
            ahead = first_half(*after) if after else None
            second_half(*held)
            held = ahead
        return carry

    lax.fori_loop(0, own // PAIR, attend, 0)

    leave = [
        pltpu.make_async_copy(att_ref, att_hbm, out_sem.at[0]),
        pltpu.make_async_copy(gq_ref, gq_hbm, out_sem.at[1]),
    ]
    last = pl.ds(remote, own)
    keys[last] = gkeys[last].astype(jnp.bfloat16)
    values[last] = gvalues[last].astype(jnp.bfloat16)
    leave += [
        pltpu.make_async_copy(keys.at[last], own_gk_hbm, out_sem.at[2]),
        pltpu.make_async_copy(values.at[last], own_gv_hbm, out_sem.at[3]),
    ]
    for copy in leave:
        copy.start()

    def send_back(i, carry):
        first = pl.ds(i * per, per)
        grad_k = gkeys[first].astype(jnp.bfloat16)
        grad_v = gvalues[first].astype(jnp.bfloat16)
        keys[first] = grad_k
        values[first] = grad_v
        for copy in grad_copies(i):
            copy.start()
        back = dot_nt(grad_k.reshape(ROWS, dim), wkv_ref[:, :dim]) + dot_nt(
            grad_v.reshape(ROWS, dim), wkv_ref[:, dim:]
        )
        far_ref[first] = back.astype(jnp.bfloat16).reshape(per, BS, dim)
        back_copy(i).start()
        return carry

    lax.fori_loop(0, chunks, send_back, 0)
    for i in range(chunks):
        leave += grad_copies(i) + [back_copy(i)]
    for copy in leave:
        copy.wait()


def layer_call(entries, counts, far, own_k, own_v, wkv, queries, ups, scaling):
    parts, _, _, dim = far.shape
    rows = queries.shape[0]
    own = rows // BS
    table = parts * CAP + own
    chunks = parts * CAP * BS // ROWS
    head = jnp.arange(HALF, dtype=jnp.int32) // BS
    diag = (head[:, None] == head[None, :]).astype(jnp.bfloat16)
    anywhere = pl.BlockSpec(memory_space=pl.ANY)
    return pl.pallas_call(
        functools.partial(layer_kernel, scaling),
        grid_spec=pltpu.PrefetchScalarGridSpec(
            num_scalar_prefetch=2,
            grid=(1,),
            in_specs=[anywhere] * 6 + [pl.BlockSpec((HALF, HALF), lambda i, *_: (0, 0))],
            out_specs=[anywhere] * 7,
            scratch_shapes=[
                pltpu.VMEM((parts * CAP, BS, dim), jnp.bfloat16),
                pltpu.VMEM((dim, 2 * dim), jnp.bfloat16),
                pltpu.VMEM((rows, dim), jnp.bfloat16),
                pltpu.VMEM((rows, dim), jnp.bfloat16),
                pltpu.VMEM((rows, dim), jnp.bfloat16),
                pltpu.VMEM((rows, dim), jnp.bfloat16),
                pltpu.VMEM((table, BS, dim), jnp.bfloat16),
                pltpu.VMEM((table, BS, dim), jnp.bfloat16),
                pltpu.VMEM((table, BS, dim), jnp.float32),
                pltpu.VMEM((table, BS, dim), jnp.float32),
                pltpu.SemaphoreType.DMA((chunks,)),
                pltpu.SemaphoreType.DMA((5,)),
                pltpu.SemaphoreType.DMA((4,)),
                pltpu.SemaphoreType.DMA((2, chunks)),
            ],
        ),
        out_shape=[
            jax.ShapeDtypeStruct((rows, dim), jnp.bfloat16),
            jax.ShapeDtypeStruct((rows, dim), jnp.bfloat16),
            jax.ShapeDtypeStruct((parts * CAP, BS, dim), jnp.bfloat16),
            jax.ShapeDtypeStruct((parts * CAP, BS, dim), jnp.bfloat16),
            jax.ShapeDtypeStruct((own, BS, dim), jnp.bfloat16),
            jax.ShapeDtypeStruct((own, BS, dim), jnp.bfloat16),
            jax.ShapeDtypeStruct(far.shape, jnp.bfloat16),
        ],
        compiler_params=pltpu.CompilerParams(vmem_limit_bytes=60 * 2**20),
    )(entries, counts, far, own_k, own_v, wkv, queries, ups, diag)


def weights_kernel(
    steps_far, core, far_ref, gk_ref, gv_ref, own_gk_ref, own_gv_ref, own_ref, gq_ref, att_ref, cot_ref, mine_ref, give_ref, terms
):
    step = pl.program_id(0)
    rows, dim = own_ref.shape

    @pl.when(step < steps_far)
    def _():
        far = far_ref[...].reshape(ROWS, dim)
        from_k = dot_tn(far, gk_ref[...].reshape(ROWS, dim))
        from_v = dot_tn(far, gv_ref[...].reshape(ROWS, dim))

        @pl.when(step == 0)
        def _():
            terms[2] = from_k
            terms[3] = from_v

        @pl.when(step > 0)
        def _():
            terms[2] += from_k
            terms[3] += from_v

    @pl.when(step == steps_far)
    def _():
        own = own_ref[...]
        terms[0] = dot_tn(own, gq_ref[...])
        terms[1] = dot_tn(att_ref[...], cot_ref[...])
        terms[2] += dot_tn(own, own_gk_ref[...])
        terms[3] += dot_tn(own, own_gv_ref[...])
        mine_ref[...] = terms[pl.ds(2 * core[0], 2)]
        give_ref[...] = terms[pl.ds(2 - 2 * core[0], 2)].astype(jnp.bfloat16)


def weights_call(core, far, grad_k, grad_v, own_gk, own_gv, own, grad_q, attended, cot):
    rows, dim = own.shape
    steps_far = far.shape[0] * CAP * BS // ROWS
    half = steps_far // CAP
    per = ROWS // BS

    def at_far(i, *_):
        chunk = jnp.minimum(i, steps_far - 1)
        return (chunk % half, chunk // half, 0, 0)

    def whole(shape):
        return pl.BlockSpec(shape, lambda i, *_: (0,) * len(shape), pipeline_mode=pl.Buffered(1))

    return pl.pallas_call(
        functools.partial(weights_kernel, steps_far),
        grid_spec=pltpu.PrefetchScalarGridSpec(
            num_scalar_prefetch=1,
            grid=(steps_far + 1,),
            in_specs=[
                pl.BlockSpec((per, None, BS, dim), at_far),
                pl.BlockSpec((per, BS, dim), lambda i, *_: (jnp.minimum(i, steps_far - 1), 0, 0)),
                pl.BlockSpec((per, BS, dim), lambda i, *_: (jnp.minimum(i, steps_far - 1), 0, 0)),
                whole((rows, dim)),
                whole((rows, dim)),
                whole((rows, dim)),
                whole((rows, dim)),
                whole((rows, dim)),
                whole((rows, dim)),
            ],
            out_specs=[whole((2, dim, dim)), whole((2, dim, dim))],
            scratch_shapes=[pltpu.VMEM((4, dim, dim), jnp.float32)],
        ),
        out_shape=[
            jax.ShapeDtypeStruct((2, dim, dim), jnp.float32),
            jax.ShapeDtypeStruct((2, dim, dim), jnp.bfloat16),
        ],
        compiler_params=pltpu.CompilerParams(vmem_limit_bytes=60 * 2**20),
        cost_estimate=pl.CostEstimate(flops=11 * 10**9, bytes_accessed=20 * 10**6, transcendentals=0),
    )(core, far, grad_k, grad_v, own_gk, own_gv, own, grad_q, attended, cot)


def combine_kernel(per, send_ref, base_ref, returned_ref, out_ref, acc):
    step = pl.program_id(0)

    @pl.when(step == 0)
    def _():
        acc[...] = base_ref[...]

    for i in range(per):
        for c in range(CAP):
            acc[send_ref[c, step * per + i]] += returned_ref[i, c].astype(jnp.float32)

    @pl.when(step == pl.num_programs(0) - 1)
    def _():
        out_ref[...] = acc[...].astype(jnp.bfloat16)


def combine_call(send, base, returned):
    blocks, _, dim = base.shape
    parts = returned.shape[0]
    per = 16
    return pl.pallas_call(
        functools.partial(combine_kernel, per),
        grid_spec=pltpu.PrefetchScalarGridSpec(
            num_scalar_prefetch=1,
            grid=(parts // per,),
            in_specs=[
                pl.BlockSpec((blocks, BS, dim), lambda i, *_: (0, 0, 0)),
                pl.BlockSpec((per, CAP, BS, dim), lambda i, *_: (i, 0, 0, 0)),
            ],
            out_specs=pl.BlockSpec((blocks, BS, dim), lambda i, *_: (0, 0, 0)),
            scratch_shapes=[pltpu.VMEM((blocks, BS, dim), jnp.float32)],
        ),
        out_shape=jax.ShapeDtypeStruct((blocks, BS, dim), jnp.bfloat16),
        compiler_params=pltpu.CompilerParams(vmem_limit_bytes=32 * 2**20),
    )(send, base, returned)


def over_cores_and_planes(mine, give, nparts):
    half = mine + lax.ppermute(give, "verts", [(v, v ^ 1) for v in range(nparts)]).astype(jnp.float32)
    planes = lax.axis_size("dp")
    here = lax.axis_index("dp")
    rows = half.shape[1] // planes
    total = lax.dynamic_slice_in_dim(half, here * rows, rows, 1)
    for d in range(1, planes):
        there = lax.dynamic_slice_in_dim(half, (here + d) % planes * rows, rows, 1)
        move = [(z, (z + d) % planes) for z in range(planes)]
        total += lax.ppermute(there.astype(jnp.bfloat16), "dp", move).astype(jnp.float32)
    return total


def moved(nparts, dx, dy):
    side = math.isqrt(nparts // 2)
    wide = nparts // side

    def go(i, d):
        return d(i) if callable(d) else (i + d) % side

    return [
        (v, go(v // wide, dy) * wide + go(v % wide // 2, dx) * 2 + v % 2) for v in range(nparts)
    ]


def ring_parts(value, nparts, along_x):
    side = math.isqrt(nparts // 2)
    moves = [moved(nparts, d, 0) if along_x else moved(nparts, 0, d) for d in range(1, side)]
    return [lax.ppermute(value, "verts", move) for move in moves]


def ring_sum(value, parts):
    one, two, three = [part.astype(jnp.float32) for part in parts]
    return ((value.astype(jnp.float32) + two) + (one + three)).astype(jnp.bfloat16)


def pair_sum(value, nparts, partner, along_x):
    move = moved(nparts, partner, 0) if along_x else moved(nparts, 0, partner)
    return value.astype(jnp.float32) + lax.ppermute(value, "verts", move).astype(jnp.float32)


def local(feats, weights, grad_out, neighbours, valid):
    nparts = lax.axis_size("verts")
    me = lax.axis_index("verts")
    _, rows, dim = feats.shape
    blocks = rows // BS
    scaling = 1.0 / math.sqrt(dim // H)
    part_ids = jnp.arange(nparts, dtype=jnp.int32)
    inputs_now = feats[0]
    cotangent = grad_out[0]
    w_kv = jnp.concatenate([weights[1], weights[2]], axis=1)

    theirs = neighbours.reshape(nparts, blocks * NNB)
    mine = (theirs // blocks == me) & (part_ids[:, None] != me)
    place = theirs % blocks
    low = jnp.min(jnp.where(mine, place, blocks), axis=1)
    high = jnp.max(jnp.where(mine, place, -1), axis=1)
    send = jnp.stack([low % blocks, jnp.maximum(high, 0)])

    lists = lax.dynamic_slice_in_dim(neighbours, me * blocks, blocks, 0).reshape(-1)
    owner = lists // blocks
    named = owner[:, None] == part_ids[None, :]
    lower = jnp.min(jnp.where(named, (lists % blocks)[:, None], blocks), axis=0)
    slot = (jnp.sum(jnp.where(named, lower[None, :], 0), axis=1) != lists % blocks).astype(jnp.int32)
    entries = jnp.where(owner == me, nparts * CAP + lists % blocks, slot * nparts + owner)
    counts = jnp.sum(valid, axis=1)[lists]

    far = lax.all_to_all(
        inputs_now.reshape(blocks, BS, dim)[send.T.reshape(-1)].reshape(nparts, CAP, BS, dim),
        "verts",
        split_axis=0,
        concat_axis=0,
        tiled=True,
    )

    queries = dot(inputs_now, weights[0]).astype(jnp.bfloat16)
    ups = dot_nt(cotangent, weights[3]).astype(jnp.bfloat16)
    own_k = dot(inputs_now, weights[1]).astype(jnp.bfloat16).reshape(blocks, BS, dim)
    own_v = dot(inputs_now, weights[2]).astype(jnp.bfloat16).reshape(blocks, BS, dim)

    attended, grad_q, grad_k, grad_v, own_gk, own_gv, back = layer_call(
        entries, counts, far, own_k, own_v, w_kv, queries, ups, scaling
    )
    own_gk, own_gv = own_gk.reshape(rows, dim), own_gv.reshape(rows, dim)
    returned = lax.all_to_all(back, "verts", split_axis=0, concat_axis=0, tiled=True)
    mine, give = weights_call(
        (me % 2).reshape(1),
        far,
        grad_k,
        grad_v,
        own_gk,
        own_gv,
        inputs_now,
        grad_q,
        attended,
        cotangent,
    )
    total = over_cores_and_planes(mine, give, nparts)
    attn_out = dot(attended, weights[3]).astype(jnp.bfloat16)
    base = dot_nt(grad_q, weights[0]) + dot_nt(own_gk, weights[1]) + dot_nt(own_gv, weights[2])
    total, attn_out, base = lax.optimization_barrier((total, attn_out, base))

    side = math.isqrt(nparts // 2)
    one, two = total[0].astype(jnp.bfloat16), total[1].astype(jnp.bfloat16)
    parts_one, parts_two, returned = lax.optimization_barrier(
        (ring_parts(one, nparts, True), ring_parts(two, nparts, False), returned)
    )
    one, two = ring_sum(one, parts_one), ring_sum(two, parts_two)
    grad_feats = combine_call(send, base.reshape(blocks, BS, dim), returned)
    one = pair_sum(one, nparts, lambda i: i ^ 1, False).astype(jnp.bfloat16)
    two = pair_sum(two, nparts, lambda i: i ^ 1, True).astype(jnp.bfloat16)
    one, two, grad_feats = lax.optimization_barrier((one, two, grad_feats))
    one = pair_sum(one, nparts, lambda i: side - 1 - i, False)
    two = pair_sum(two, nparts, lambda i: side - 1 - i, True)
    half = jnp.stack([one, two])
    other = lax.ppermute(half, "verts", [(v, v ^ 1) for v in range(nparts)])
    first = me % 2 == 0
    q_o = jnp.where(first, half, other)
    k_v = jnp.where(first, other, half)
    grad_weights = jnp.concatenate([q_o[:1], k_v, q_o[1:]], axis=0)
    return (attn_out[None], grad_feats.reshape(1, rows, dim), grad_weights)


def solution(mesh):
    in_specs = (P("dp", "verts", None), P(), P("dp", "verts", None), P(), P())
    out_specs = (P("dp", "verts", None), P("dp", "verts", None), P(None, "dp", None))
    return jax.shard_map(local, mesh=mesh, in_specs=in_specs, out_specs=out_specs, check_vma=False)
```
